128 devices in a mesh: seq: 32 (over z, y, core), head: 4 (over x).
Axes of the slice: x: 4, y: 4, z: 4, core: 2. Of those that a mesh axis runs over, the one named last changes fastest.
Arguments:
- hidden_in: bfloat16 [64, 8192], P(None, 'seq'), may hold values from -6 to 6
- w_query: bfloat16 [8192, 8192], P('seq', 'head'), may hold values from -0.0625 to 0.0625
- w_keyval: bfloat16 [8192, 2048], P('seq', 'head'), may hold values from -0.0625 to 0.0625
- w_out: bfloat16 [8192, 8192], P('head', 'seq'), may hold values from -0.0625 to 0.0625
- key_cache: bfloat16 [4096, 128, 1024], P('seq', None, 'head'), may hold values from -6 to 6
- value_cache: bfloat16 [4096, 128, 1024], P('seq', None, 'head'), may hold values from -6 to 6
- key_scale: float32 [4096, 8], P('seq', 'head'), may hold values from 0.25 to 300
- value_scale: float32 [4096, 8], P('seq', 'head'), may hold values from 0.5 to 2
- page_counts: int32 [64], replicated, may hold values from 1 to 512, 4096 in all
- slot_pages: int32 [4096], P('seq'), may hold values from 0 to 4095, each once
- trim: int32 [64], replicated, may hold values from 0 to 127
Outputs:
- attn_out: bfloat16 [64, 8192], P(None, 'seq')
The draws below stay inside these ranges and needn't reach their ends.
Inputs may be any that keep to these rules, and one draw needn't show every extreme that they name: `page_counts`: every request has at least one page; the page counts sum to 4096.
All inputs are finite; a program needn't handle non-finite values.
Results may differ from the reference program's by a relative error of at most 0.0095.
Values may be sent and summed in bfloat16 or wider, within the bound.
A program may use at most 128 MiB of HBM per device.

```python
import math
import jax
import jax.numpy as jnp
import numpy as np
from jax import lax

D = 8192
QH = 64
KEY_VALUE_HEADS = 8
HD = 128
PAGE = 128
PAGES_DEV = 128
REQ = 64
TOTAL_PAGE_SLOTS = 4096
MOSTP = 512


def draw_key_scale(key, part):
    key = jax.random.fold_in(key, 7)
    start_offset = jnp.exp(jax.random.uniform(key, (TOTAL_PAGE_SLOTS, KEY_VALUE_HEADS), jnp.float32, math.log(0.25), math.log(2.0)))
    return start_offset


def touch_ends(array, stream_key, low, top_value):
    dims = array.shape
    spot = [jax.random.randint(jax.random.fold_in(stream_key, axis), (), 0, dims[axis]) for axis in range(len(dims))]
    array = array.at[tuple(spot)].set(low)
    longest = dims.index(max(dims))
    spot[longest] = (spot[longest] + 1) % dims[longest]
    return array.at[tuple(spot)].set(top_value)


def level_of(rng, extent, pieces, least, largest):
    factor_of, own = 1.0, jax.random.fold_in(rng, 6)
    for position, blocks in pieces:
        steps = jnp.exp(jax.random.uniform(jax.random.fold_in(own, position), (blocks,), jnp.float32, least / len(pieces), largest / len(pieces)))
        factor_of = factor_of * jnp.repeat(steps, extent[position] // blocks).reshape([-1 if axis == position else 1 for axis in range(len(extent))])
    return factor_of


def split_up(amount, total, bound, lean):
    loads = [(1 << 20) // math.isqrt(standing ** lean) + 1 for standing in range(2, amount + 1)]
    rest, given = total - bound - (amount - 1), [1] * (amount - 1)
    while rest > 0:
        candidates = [i for i in range(amount - 1) if given[i] < bound]
        mass, budget = sum([loads[i] for i in candidates]), rest
        for i in candidates:
            more = min(bound - given[i], max(1, budget * loads[i] // mass), rest)
            given[i] = given[i] + more
            rest = rest - more
    return np.array([bound] + given)


def ragged(own_key, count, total, limit, skew):
    if count == 2:
        one = jax.random.randint(own_key, (), max(1, total - limit), min(limit, total - 1) + 1)
        return jnp.stack([one, total - one])
    sizes = jnp.asarray(split_up(count, total, limit, skew), jnp.int32)
    couples = (count - 1) // 2
    source_of, taker = sizes[1:1 + 2 * couples:2], sizes[2:2 + 2 * couples:2]
    margin = jnp.minimum(source_of - 1, limit - taker)
    passed = jax.random.randint(jax.random.fold_in(own_key, 1), (couples,), 0, 1 << 20) % (margin + 1)
    sizes = sizes.at[1:1 + 2 * couples:2].set(source_of - passed).at[2:2 + 2 * couples:2].set(taker + passed)
    return sizes[jax.random.permutation(jax.random.fold_in(own_key, 2), count)]


def noise(key, dims, scale, limit, cuts=(), held_as=jnp.bfloat16):
    loudness = level_of(key, dims, cuts, -0.22, 0.18) if cuts else 1.0
    result = jax.random.normal(key, dims, jnp.float32) * scale * loudness
    return jnp.minimum(jnp.maximum(result, -limit), limit).astype(held_as)


def setup_inputs(seed: int = 0) -> dict:
    seeds = jax.random.split(jax.random.key(seed), 12)
    hidden_in = noise(seeds[0], (REQ, D), 1.0, 6.0, ((1, 32),))
    w_query = noise(seeds[1], (D, QH * HD), D ** -0.5, 0.0625, ((0, 32), (1, 4)))
    w_keyval = noise(seeds[2], (D, 2 * KEY_VALUE_HEADS * HD), D ** -0.5, 0.0625, ((0, 32), (1, 4)))
    w_out = noise(seeds[3], (QH * HD, D), (QH * HD) ** -0.5, 0.0625, ((0, 4), (1, 32)))
    key_cache = noise(seeds[4], (TOTAL_PAGE_SLOTS, PAGE, KEY_VALUE_HEADS * HD), 1.0, 6.0, ((0, 32), (2, 4)))
    value_cache = noise(seeds[5], (TOTAL_PAGE_SLOTS, PAGE, KEY_VALUE_HEADS * HD), 1.0, 6.0, ((0, 32), (2, 4)))
    key_scale = draw_key_scale(jax.random.fold_in(seeds[11], 71), 0)
    value_scale = jnp.clip(jnp.exp(math.log(2.0) - 1.3862944 * jax.random.uniform(seeds[7], (TOTAL_PAGE_SLOTS, KEY_VALUE_HEADS), jnp.float32) ** level_of(seeds[7], (TOTAL_PAGE_SLOTS, KEY_VALUE_HEADS), ((0, 32), (1, 4)), -0.2, 0.2)), 0.5, 2.0)
    page_counts = ragged(seeds[8], REQ, TOTAL_PAGE_SLOTS, MOSTP, 2).astype(jnp.int32)
    slot_pages = jax.random.permutation(seeds[9], TOTAL_PAGE_SLOTS).astype(jnp.int32)
    trim = touch_ends(jax.random.randint(seeds[10], (REQ,), 0, PAGE), jax.random.fold_in(seeds[10], 1), 0, PAGE - 1).astype(jnp.int32)
    return {"hidden_in": hidden_in, "w_query": w_query, "w_keyval": w_keyval, "w_out": w_out, "key_cache": key_cache, "value_cache": value_cache, "key_scale": key_scale, "value_scale": value_scale, "page_counts": page_counts, "slot_pages": slot_pages, "trim": trim}


masked_low = -1e+30

def page_table(page_counts, slot_pages, trim):
    start = jnp.cumsum(page_counts) - page_counts
    ends = start + page_counts
    owner = lax.optimization_barrier(jnp.sum((ends[None, :] <= slot_pages[:, None]).astype(jnp.int32), axis=1)).astype(jnp.int32)
    index = (slot_pages - start[owner]).astype(jnp.int32)
    length = (PAGE * page_counts - trim).astype(jnp.int32)
    return (owner, index, length[owner])

def reference(hidden_in, w_query, w_keyval, w_out, key_cache, value_cache, key_scale, value_scale, page_counts, slot_pages, trim):
    group = QH // KEY_VALUE_HEADS
    query = jnp.dot(hidden_in, w_query, preferred_element_type=jnp.float32).astype(jnp.bfloat16)
    keyval = jnp.dot(hidden_in, w_keyval, preferred_element_type=jnp.float32).astype(jnp.bfloat16)
    owner, index, page_len = page_table(page_counts, slot_pages, trim)
    inverse_square_root = 1.0 / math.sqrt(HD)
    query_heads = query.reshape(REQ, KEY_VALUE_HEADS, group, HD)

    def block(input_arrays):
        key_rows, value_rows, key_page_scale, value_page_scale, owner_identifiers, slot_index, page_length = input_arrays
        q_sel = query_heads[owner_identifiers].astype(jnp.float32)
        unscaled_pages = jnp.einsum('sgjd,stgd->sgjt', q_sel, key_rows.reshape(-1, PAGE, KEY_VALUE_HEADS, HD).astype(jnp.float32))
        score_matrix = unscaled_pages * (key_page_scale * inverse_square_root)[:, :, None, None]
        pos = slot_index[:, None] * PAGE + jnp.arange(PAGE, dtype=jnp.int32)[None, :]
        valid = (pos < page_length[:, None])[:, None, None, :]
        score_matrix = jnp.where(valid, score_matrix, masked_low)
        pmax = lax.optimization_barrier(jnp.max(score_matrix, axis=-1))
        probs = jnp.where(valid, jnp.exp(score_matrix - pmax[..., None]), 0.0).astype(jnp.bfloat16)
        psum = lax.optimization_barrier(jnp.sum(probs.astype(jnp.float32), axis=-1))
        pout = jnp.einsum('sgjt,stgd->sgjd', probs.astype(jnp.float32), value_rows.reshape(-1, PAGE, KEY_VALUE_HEADS, HD).astype(jnp.float32))
        pout = pout * value_page_scale[:, :, None, None]
        count = key_rows.shape[0]
        return (pmax.reshape(count, QH), psum.reshape(count, QH), pout.reshape(count, QH * HD))
    nblk = TOTAL_PAGE_SLOTS // PAGES_DEV

    def split(a):
        return a.reshape((nblk, PAGES_DEV) + a.shape[1:])
    pmax, psum, pout = lax.map(block, (split(key_cache), split(value_cache), split(key_scale), split(value_scale), split(owner), split(index), split(page_len)))
    pmax = pmax.reshape(TOTAL_PAGE_SLOTS, QH)
    psum = psum.reshape(TOTAL_PAGE_SLOTS, QH)
    pout = pout.reshape(TOTAL_PAGE_SLOTS, QH * HD)
    onehot = owner[None, :] == jnp.arange(REQ, dtype=jnp.int32)[:, None]
    cache_max = lax.optimization_barrier(jnp.max(jnp.where(onehot[:, :, None], pmax[None, :, :], masked_low), axis=1))
    weight = jnp.exp(pmax - cache_max[owner])
    cache_sum = jax.ops.segment_sum(psum * weight, owner, num_segments=REQ)
    cache_out = jax.ops.segment_sum((pout.reshape(TOTAL_PAGE_SLOTS, QH, HD) * weight[:, :, None]).reshape(TOTAL_PAGE_SLOTS, QH * HD), owner, num_segments=REQ)
    kv = keyval.reshape(REQ, KEY_VALUE_HEADS, 2, HD).astype(jnp.float32)
    new_key = kv[:, :, 0]
    new_value = kv[:, :, 1]
    own = jnp.einsum('rgjd,rgd->rgj', query_heads.astype(jnp.float32), new_key).reshape(REQ, QH) * inverse_square_root
    top = jnp.maximum(cache_max, own)
    old_part = jnp.exp(cache_max - top)
    new_part = jnp.exp(own - top)
    denom = cache_sum * old_part + new_part
    spread_value = jnp.broadcast_to(new_value[:, :, None, :], (REQ, KEY_VALUE_HEADS, group, HD)).reshape(REQ, QH, HD)
    numer = cache_out.reshape(REQ, QH, HD) * old_part[:, :, None] + new_part[:, :, None] * spread_value
    context = (numer / denom[:, :, None]).reshape(REQ, QH * HD).astype(jnp.bfloat16)
    return jnp.dot(context, w_out, preferred_element_type=jnp.float32).astype(jnp.bfloat16)
```

```python
import functools
import math

import jax
import jax.numpy as jnp
from jax import lax
from jax.experimental import pallas as pl
from jax.experimental.pallas import tpu as pltpu
from jax.sharding import PartitionSpec as P

HD = 128
PAGE = 128
MESH = pl.DeviceIdType.MESH
masked_low = -1e30
f32 = jnp.float32
bf16 = jnp.bfloat16
inverse_square_root = 1.0 / math.sqrt(HD)


def each(low, high, step, unroll=1):
    def run(k, carry):
        step(k)
        return carry

    lax.fori_loop(low, high, run, 0, unroll=unroll)


def project(hid, wq, wkv, part):
    x = hid[...]
    for h in range(0, 16, 2):
        y = jnp.dot(x, wq[:, h * HD : (h + 2) * HD], preferred_element_type=f32)
        for c in range(2):
            for j in range(2):
                part[c, h + j, 0:32] = y[32 * c : 32 * c + 32, HD * j : HD * j + HD]
    for b in range(0, 4, 2):
        y = jnp.dot(x, wkv[:, b * HD : (b + 2) * HD], preferred_element_type=f32)
        for c in range(2):
            for j in range(2):
                for rows in range(4):
                    at = 32 * c + 8 * rows
                    part[c, rows * 4 + b + j, 32:40] = y[at : at + 8, HD * j : HD * j + HD]


def iota(shape, axis):
    return lax.broadcasted_iota(jnp.int32, shape, axis)


def page_table(cnt, slt, trm, ksv, sel, selt, nv, ks0, ks1):
    zeros = jnp.zeros((1, 64), f32)
    count = jnp.concatenate([cnt[...].astype(f32), zeros], axis=1)
    trim = jnp.concatenate([trm[...].astype(f32), zeros], axis=1)
    i, j = iota((128, 128), 0), iota((128, 128), 1)
    count_col = jnp.sum(jnp.where(i == j, count, 0.0), axis=1, keepdims=True)
    end_col = jnp.sum(jnp.where(j <= i, count, 0.0), axis=1, keepdims=True)
    end = jnp.sum(jnp.where(i <= j, count_col, 0.0), axis=0, keepdims=True)
    start, start_col = end - count, end_col - count_col
    page = slt[...].astype(f32)
    page_col = jnp.sum(jnp.where(i == j, page, 0.0), axis=1, keepdims=True)
    mine = (start <= page_col) & (page_col < end)
    sel[...] = jnp.where(mine, 1.0, 0.0)
    selt[...] = jnp.where((start_col <= page) & (page < end_col), 1.0, 0.0)[:64].astype(bf16)
    left = PAGE * count - trim - PAGE * (page_col - start)
    valid = jnp.sum(jnp.where(mine, left, 0.0), axis=1, keepdims=True)
    nv[...] = jnp.broadcast_to(valid, (128, 128))
    ks0[...] = jnp.broadcast_to(ksv[:, 0:1] * inverse_square_root, (128, 128))
    ks1[...] = jnp.broadcast_to(ksv[:, 1:2] * inverse_square_root, (128, 128))


def select_query(qall, sel, qs):
    onehot = sel[:, 0:64].astype(bf16)
    for h in range(16):
        q = qall[2 * h : 2 * h + 2].reshape(64, HD)
        qs[h * 128 : (h + 1) * 128] = jnp.dot(onehot, q, preferred_element_type=f32)


def attend(slot, kc, vc, qs, nv, ks0, ks1, po, pm, ps):
    q = qs[pl.ds(slot, 16, stride=128), :]
    none = jnp.zeros((8, HD), f32)
    left = jnp.concatenate([q[0:8], none], axis=0).astype(bf16)
    right = jnp.concatenate([none, q[8:16]], axis=0).astype(bf16)
    query = jnp.concatenate([left, right], axis=1)
    score = lax.dot_general(query, kc[slot], (((1,), (1,)), ((), ())), preferred_element_type=f32)
    scale0 = jnp.broadcast_to(ks0[pl.ds(slot, 1), :], (8, PAGE))
    scale1 = jnp.broadcast_to(ks1[pl.ds(slot, 1), :], (8, PAGE))
    score = score * jnp.concatenate([scale0, scale1], axis=0)
    tokens = jnp.broadcast_to(nv[pl.ds(slot, 1), :], (16, PAGE))
    valid = iota((16, PAGE), 1).astype(f32) < tokens
    score = jnp.where(valid, score, masked_low)
    top = jnp.max(score, axis=1, keepdims=True)
    probs = jnp.where(valid, jnp.exp(score - top), 0.0).astype(bf16)
    total = jnp.sum(probs.astype(f32), axis=1, keepdims=True)
    out = jnp.dot(probs, vc[slot], preferred_element_type=f32)
    at = pl.ds(pl.multiple_of(slot * 16, 16), 16)
    po[at, :] = jnp.concatenate([out[0:8, 0:HD], out[8:16, HD : 2 * HD]], axis=0)
    pm[at, :] = jnp.broadcast_to(top, (16, HD))
    ps[at, :] = jnp.broadcast_to(total, (16, HD))


def three(x):
    a = x.astype(bf16).astype(f32)
    b = (x - a).astype(bf16).astype(f32)
    return a, b, x - a - b


def fold(h, sel, selt, vsv, po, pm, ps, msg):
    rows = pl.ds(h, 128, stride=16)
    mine = sel[...] > 0.5
    page_max = pm[rows, :]
    dev_max = jnp.max(jnp.where(mine, page_max, masked_low), axis=0, keepdims=True)
    slot_max = jnp.max(jnp.where(mine, dev_max, masked_low), axis=1, keepdims=True)
    weight = jnp.exp(page_max - slot_max)
    dev_sum = jnp.sum(jnp.where(mine, ps[rows, :] * weight, 0.0), axis=0, keepdims=True)
    g = h // 8
    weighted = (po[rows, :] * (weight * vsv[:, g : g + 1])).astype(bf16)
    dev_out = jnp.dot(selt[...], weighted, preferred_element_type=f32).astype(bf16)
    row = iota((16, 128), 0)
    stats = jnp.zeros((16, 128), f32)
    for at, part in enumerate(three(dev_max) + three(dev_sum)):
        stats = jnp.where(row == at, part, stats)
    stats = stats.astype(bf16)
    for c in range(2):
        msg[2 * h + c, 0:32] = dev_out[32 * c : 32 * c + 32]
        msg[2 * h + c, 32:48] = stats


def finish(chip, core, rmsg, qown, kvall, flat, turned):
    flat[...] = jnp.zeros((128, 128), f32)
    maxes, sums = [], []
    for i in range(32):
        stats = rmsg[i, 32:48].astype(f32)
        maxes.append(stats[0:1] + stats[1:2] + stats[2:3])
        sums.append(stats[3:4] + stats[4:5] + stats[5:6])
    maxes = jnp.concatenate(maxes, axis=0)
    sums = jnp.concatenate(sums, axis=0)
    cache_max = jnp.max(maxes, axis=0, keepdims=True)
    factors = jnp.exp(maxes - cache_max)
    flat[0:32] = factors
    flat[32:33] = cache_max
    flat[33:34] = jnp.sum(sums * factors, axis=0, keepdims=True)
    turned[...] = flat[...].T
    cols = turned[pl.ds(pl.multiple_of(core * 32, 32), 32), :]
    cache_out = jnp.zeros((32, HD), f32)
    for i in range(32):
        cache_out = cache_out + cols[:, i : i + 1] * rmsg[i, 0:32].astype(f32)
    cache_max, cache_sum = cols[:, 32:33], cols[:, 33:34]
    at = chip // 8 * 2
    new_key = jnp.concatenate([kvall[4 * r + at] for r in range(4)], axis=0)
    new_value = jnp.concatenate([kvall[4 * r + at + 1] for r in range(4)], axis=0)
    own = jnp.sum(qown[...].astype(f32) * new_key, axis=1, keepdims=True) * inverse_square_root
    top = jnp.maximum(cache_max, own)
    old_part = jnp.exp(cache_max - top)
    new_part = jnp.exp(own - top)
    denom = cache_sum * old_part + new_part
    return ((cache_out * old_part + new_part * new_value) / denom).astype(bf16)


def kernel(
    hidden_in, w_query, w_keyval, w_out, key_cache, value_cache, key_scale, value_scale, page_counts, slot_pages, trim,
    out_ref,
    hid, wq, wkv, wo, kc, vc, ksv, vsv, cnt, slt, trm,
    part, sib, rsb, qown, kvown, qall, kvall, qs, po, pm, ps, sel, selt, nv, ks0, ks1,
    msg, rmsg, flat, turned, ctx_own, ctx_all, xsend, xrecv,
    load_sem, sib_sem, rs_send, rs_recv, q_send, q_recv, kv_send, kv_recv, o_send, o_recv, c_send, c_recv, x_send, x_recv,
):
    me, col = lax.axis_index("seq"), lax.axis_index("head")
    chip, core = me // 2, lax.rem(me, 2)
    sibling = me + 1 - 2 * core

    barrier = pltpu.get_barrier_semaphore()

    def greet(k):
        pl.semaphore_signal(barrier, inc=1, device_id=(lax.rem(me + k, 32), col), device_id_type=MESH)

    def greet_column(k):
        pl.semaphore_signal(barrier, inc=1, device_id=(me, lax.rem(col + k, 4)), device_id_type=MESH)

    each(1, 32, greet)
    each(1, 4, greet_column)

    def load(k, source, target):
        copy = pltpu.make_async_copy(source, target, load_sem.at[k])
        copy.start()
        return copy

    first = [load(0, hidden_in, hid), load(1, w_query, wq), load(2, w_keyval, wkv)]
    small = [
        load(3, page_counts, cnt), load(4, slot_pages, slt), load(5, trim, trm),
        load(6, key_scale, ksv), load(7, value_scale, vsv),
    ]
    for copy in first:
        copy.wait()
    keys, values, outs = load(8, key_cache, kc), load(9, value_cache, vc), load(10, w_out, wo)
    project(hid, wq, wkv, part)

    def send(source, target, send_sem, recv_sem, device):
        return pltpu.make_async_remote_copy(
            source, target, send_sem, recv_sem, device_id=device, device_id_type=MESH
        )

    pl.semaphore_wait(barrier, 34)
    swap = send(part.at[1 - core], sib, sib_sem.at[0], sib_sem.at[1], (sibling, col))
    swap.start()
    for copy in small:
        copy.wait()
    page_table(cnt, slt, trm, ksv, sel, selt, nv, ks0, ks1)
    swap.wait()
    sib[...] += part[core]

    def reduce_copy(k, there):
        peer = lax.rem(chip + k, 16)
        return send(sib.at[peer], rsb.at[peer if there else chip], rs_send.at[k], rs_recv.at[peer if there else chip],
                    (2 * peer + core, col))

    each(1, 16, lambda k: reduce_copy(k, False).start())
    rsb[chip] = sib[chip]
    each(1, 16, lambda k: reduce_copy(k, True).wait_recv())
    total = rsb[0]
    for i in range(1, 16):
        total = total + rsb[i]
    qown[...] = total[0:32].astype(bf16)
    kvown[...] = total[32:40].astype(bf16).astype(f32)

    def query_copy(k, there):
        peer = lax.rem(me + k, 32)
        at = peer if there else me
        return send(qown, qall.at[at], q_send.at[k], q_recv.at[at], (peer, col))

    def keyval_copy(k, there):
        peer = lax.rem(chip + k, 16)
        at = peer if there else chip
        return send(kvown, kvall.at[at], kv_send.at[k], kv_recv.at[at], (2 * peer + core, col))

    each(1, 32, lambda k: query_copy(k, False).start())
    each(1, 16, lambda k: keyval_copy(k, False).start())
    qall[me] = qown[...]
    kvall[chip] = kvown[...]
    keys.wait()
    values.wait()
    each(1, 32, lambda k: query_copy(k, True).wait_recv())
    select_query(qall, sel, qs)

    def slots(k):
        for u in range(8):
            attend(k * 8 + u, kc, vc, qs, nv, ks0, ks1, po, pm, ps)

    each(0, 16, slots)
    for h in range(16):
        fold(h, sel, selt, vsv, po, pm, ps, msg)

    def out_copy(k, there):
        peer = lax.rem(me + k, 32)
        at = peer if there else me
        return send(msg.at[peer], rmsg.at[at], o_send.at[k], o_recv.at[at], (peer, col))

    each(1, 32, lambda k: out_copy(k, False).start())
    rmsg[me] = msg[me]
    each(1, 16, lambda k: keyval_copy(k, True).wait_recv())
    each(1, 32, lambda k: out_copy(k, True).wait_recv())
    ctx_own[...] = finish(chip, core, rmsg, qown, kvall, flat, turned)

    def context_copy(k, there):
        peer = lax.rem(me + k, 32)
        at = peer if there else me
        return send(ctx_own, ctx_all.at[at], c_send.at[k], c_recv.at[at], (peer, col))

    each(1, 32, lambda k: context_copy(k, False).start())
    ctx_all[me] = ctx_own[...]
    outs.wait()
    each(1, 32, lambda k: context_copy(k, True).wait_recv())
    context = jnp.concatenate([ctx_all[2 * h : 2 * h + 2].reshape(64, HD) for h in range(16)], axis=1)
    result = jnp.dot(context, wo[...], preferred_element_type=f32)
    xsend[...] = result.astype(bf16)

    def head_copy(k, there):
        peer = lax.rem(col + k, 4)
        at = peer if there else col
        return send(xsend, xrecv.at[at], x_send.at[k], x_recv.at[at], (me, peer))

    each(1, 4, lambda k: head_copy(k, False).start())
    each(1, 4, lambda k: head_copy(k, True).wait_recv())
    for k in range(1, 4):
        result = result + xrecv[lax.rem(col + k, 4)].astype(f32)
    out_ref[...] = result.astype(bf16)

    each(1, 16, lambda k: reduce_copy(k, True).wait_send())
    each(1, 16, lambda k: keyval_copy(k, True).wait_send())
    each(1, 32, lambda k: query_copy(k, True).wait_send())
    each(1, 32, lambda k: out_copy(k, True).wait_send())
    each(1, 32, lambda k: context_copy(k, True).wait_send())
    each(1, 4, lambda k: head_copy(k, True).wait_send())


def body(
    hidden_in, w_query, w_keyval, w_out, key_cache, value_cache, key_scale, value_scale, page_counts, slot_pages, trim
):
    vmem = pltpu.VMEM
    dma = pltpu.SemaphoreType.DMA
    return pl.pallas_call(
        kernel,
        out_shape=jax.ShapeDtypeStruct((64, 256), bf16),
        in_specs=[pl.BlockSpec(memory_space=pl.ANY)] * 11,
        out_specs=pl.BlockSpec(memory_space=pltpu.VMEM),
        scratch_shapes=[
            vmem((64, 256), bf16), vmem((256, 2048), bf16), vmem((256, 512), bf16), vmem((2048, 256), bf16),
            vmem((128, PAGE, 256), bf16), vmem((128, PAGE, 256), bf16), vmem((128, 2), f32), vmem((128, 2), f32),
            vmem((1, 64), jnp.int32), vmem((1, 128), jnp.int32), vmem((1, 64), jnp.int32),
            vmem((2, 16, 40, HD), f32), vmem((16, 40, HD), f32), vmem((16, 40, HD), f32),
            vmem((32, HD), bf16), vmem((8, HD), f32), vmem((32, 32, HD), bf16), vmem((16, 8, HD), f32),
            vmem((2048, HD), f32), vmem((2048, HD), f32), vmem((2048, HD), f32), vmem((2048, HD), f32),
            vmem((128, 128), f32), vmem((64, 128), bf16), vmem((128, 128), f32),
            vmem((128, 128), f32), vmem((128, 128), f32),
            vmem((32, 48, HD), bf16), vmem((32, 48, HD), bf16), vmem((128, 128), f32), vmem((128, 128), f32),
            vmem((32, HD), bf16), vmem((32, 32, HD), bf16), vmem((64, 256), bf16), vmem((4, 64, 256), bf16),
            dma((11,)), dma((2,)), dma((16,)), dma((16,)), dma((32,)), dma((32,)), dma((16,)), dma((16,)),
            dma((32,)), dma((32,)), dma((32,)), dma((32,)), dma((4,)), dma((4,)),
        ],
        compiler_params=pltpu.CompilerParams(collective_id=0, has_side_effects=True, vmem_limit_bytes=40 << 20),
        cost_estimate=pl.CostEstimate(flops=300_000_000, bytes_accessed=20_000_000, transcendentals=300_000),
    )(
        hidden_in, w_query, w_keyval, w_out, key_cache, value_cache, key_scale, value_scale,
        page_counts.reshape(1, 64), slot_pages.reshape(1, 128), trim.reshape(1, 64),
    )


def solution(mesh):
    return jax.shard_map(
        body,
        mesh=mesh,
        in_specs=(
            P(None, "seq"),
            P("seq", "head"),
            P("seq", "head"),
            P("head", "seq"),
            P("seq", None, "head"),
            P("seq", None, "head"),
            P("seq", "head"),
            P("seq", "head"),
            P(),
            P("seq"),
            P(),
        ),
        out_specs=P(None, "seq"),
        check_vma=False,
    )
```

```python
import functools
import math

import jax
import jax.numpy as jnp
from jax import lax
from jax.experimental import pallas as pl
from jax.experimental.pallas import tpu as pltpu
from jax.sharding import PartitionSpec as P

HD = 128
PAGE = 128
MESH = pl.DeviceIdType.MESH
masked_low = -1e30
f32 = jnp.float32
bf16 = jnp.bfloat16
inverse_square_root = 1.0 / math.sqrt(HD)


def each(low, high, step, unroll=1):
    def run(k, carry):
        step(k)
        return carry

    lax.fori_loop(low, high, run, 0, unroll=unroll)


def project(hid, wq, wkv, part):
    x = hid[...]
    for h in range(0, 16, 2):
        y = jnp.dot(x, wq[:, h * HD : (h + 2) * HD], preferred_element_type=f32)
        for c in range(2):
            for j in range(2):
                part[c, h + j, 0:32] = y[32 * c : 32 * c + 32, HD * j : HD * j + HD]
    for b in range(0, 4, 2):
        y = jnp.dot(x, wkv[:, b * HD : (b + 2) * HD], preferred_element_type=f32)
        for c in range(2):
            for j in range(2):
                for rows in range(4):
                    at = 32 * c + 8 * rows
                    part[c, rows * 4 + b + j, 32:40] = y[at : at + 8, HD * j : HD * j + HD]


def iota(shape, axis):
    return lax.broadcasted_iota(jnp.int32, shape, axis)


def page_table(cnt, slt, trm, ksv, vsv, sel, selt, nv, ks0, ks1, vs):
    zeros = jnp.zeros((1, 64), f32)
    count = jnp.concatenate([cnt[...].astype(f32), zeros], axis=1)
    trim = jnp.concatenate([trm[...].astype(f32), zeros], axis=1)
    i, j = iota((128, 128), 0), iota((128, 128), 1)
    count_col = jnp.sum(jnp.where(i == j, count, 0.0), axis=1, keepdims=True)
    end_col = jnp.sum(jnp.where(j <= i, count, 0.0), axis=1, keepdims=True)
    end = jnp.sum(jnp.where(i <= j, count_col, 0.0), axis=0, keepdims=True)
    start, start_col = end - count, end_col - count_col
    page = slt[...].astype(f32)

    def column(row):
        return jnp.sum(jnp.where(i == j, row, 0.0), axis=1, keepdims=True)

    page_col = column(page)
    mine = (start <= page_col) & (page_col < end)
    sel[...] = jnp.where(mine, 1.0, 0.0)
    selt[...] = jnp.where((start_col <= page) & (page < end_col), 1.0, 0.0)[:64].astype(bf16)
    left = PAGE * count - trim - PAGE * (page_col - start)
    valid = jnp.sum(jnp.where(mine, left, 0.0), axis=1, keepdims=True)
    nv[...] = jnp.broadcast_to(valid, (128, 128))
    ks0[...] = jnp.broadcast_to(column(ksv[0:1, :]) * inverse_square_root, (128, 128))
    ks1[...] = jnp.broadcast_to(column(ksv[1:2, :]) * inverse_square_root, (128, 128))
    for g in range(2):
        vs[g] = jnp.broadcast_to(column(vsv[g : g + 1, :]), (128, 128))


def select_query(qall, sel, qs):
    onehot = sel[:, 0:64].astype(bf16)
    for h in range(16):
        q = qall[2 * h : 2 * h + 2].reshape(64, HD)
        qs[h * 128 : (h + 1) * 128] = jnp.dot(onehot, q, preferred_element_type=f32)


def attend(slots, kc, vc, qs, nv, ks0, ks1, po, pm, ps):
    none = jnp.zeros((8, HD), f32)
    token = iota((16, PAGE), 1).astype(f32)
    scores, valids = [], []
    for slot in slots:
        q = qs[pl.ds(slot, 16, stride=128), :]
        left = jnp.concatenate([q[0:8], none], axis=0).astype(bf16)
        right = jnp.concatenate([none, q[8:16]], axis=0).astype(bf16)
        query = jnp.concatenate([left, right], axis=1)
        score = lax.dot_general(query, kc[slot], (((1,), (1,)), ((), ())), preferred_element_type=f32)
        scale0 = jnp.broadcast_to(ks0[pl.ds(slot, 1), :], (8, PAGE))
        scale1 = jnp.broadcast_to(ks1[pl.ds(slot, 1), :], (8, PAGE))
        score = score * jnp.concatenate([scale0, scale1], axis=0)
        valid = token < jnp.broadcast_to(nv[pl.ds(slot, 1), :], (16, PAGE))
        scores.append(jnp.where(valid, score, masked_low))
        valids.append(valid)
    tops = [jnp.max(score, axis=1, keepdims=True) for score in scores]
    probs = [
        jnp.where(valid, jnp.exp(score - top), 0.0).astype(bf16)
        for score, valid, top in zip(scores, valids, tops)
    ]
    totals = [jnp.sum(prob.astype(f32), axis=1, keepdims=True) for prob in probs]
    outs = [jnp.dot(prob, vc[slot], preferred_element_type=f32) for slot, prob in zip(slots, probs)]
    for slot, out, top, total in zip(slots, outs, tops, totals):
        at = pl.ds(pl.multiple_of(slot * 16, 16), 16)
        po[at, :] = jnp.concatenate([out[0:8, 0:HD], out[8:16, HD : 2 * HD]], axis=0)
        pm[at, :] = jnp.broadcast_to(top, (16, HD))
        ps[at, :] = jnp.broadcast_to(total, (16, HD))


def three(x):
    a = x.astype(bf16).astype(f32)
    b = (x - a).astype(bf16).astype(f32)
    return a, b, x - a - b


def fold(h, sel, selt, vs, po, pm, ps, msg):
    rows = pl.ds(h, 128, stride=16)
    mine = sel[...] > 0.5
    page_max = pm[rows, :]
    dev_max = jnp.max(jnp.where(mine, page_max, masked_low), axis=0, keepdims=True)
    slot_max = jnp.max(jnp.where(mine, dev_max, masked_low), axis=1, keepdims=True)
    weight = jnp.exp(page_max - slot_max)
    dev_sum = jnp.sum(jnp.where(mine, ps[rows, :] * weight, 0.0), axis=0, keepdims=True)
    g = h // 8
    weighted = (po[rows, :] * (weight * vs[g])).astype(bf16)
    dev_out = jnp.dot(selt[...], weighted, preferred_element_type=f32).astype(bf16)
    row = iota((16, 128), 0)
    stats = jnp.zeros((16, 128), f32)
    for at, part in enumerate(three(dev_max) + three(dev_sum)):
        stats = jnp.where(row == at, part, stats)
    stats = stats.astype(bf16)
    for c in range(2):
        msg[2 * h + c, 0:32] = dev_out[32 * c : 32 * c + 32]
        msg[2 * h + c, 32:48] = stats


def finish(chip, core, rmsg, qown, kvall, flat, turned):
    flat[...] = jnp.zeros((128, 128), f32)
    maxes, sums = [], []
    for i in range(32):
        stats = rmsg[i, 32:48].astype(f32)
        maxes.append(stats[0:1] + stats[1:2] + stats[2:3])
        sums.append(stats[3:4] + stats[4:5] + stats[5:6])
    maxes = jnp.concatenate(maxes, axis=0)
    sums = jnp.concatenate(sums, axis=0)
    cache_max = jnp.max(maxes, axis=0, keepdims=True)
    factors = jnp.exp(maxes - cache_max)
    flat[0:32] = factors
    flat[32:33] = cache_max
    flat[33:34] = jnp.sum(sums * factors, axis=0, keepdims=True)
    turned[...] = flat[...].T
    cols = turned[pl.ds(pl.multiple_of(core * 32, 32), 32), :]
    cache_out = jnp.zeros((32, HD), f32)
    for i in range(32):
        cache_out = cache_out + cols[:, i : i + 1] * rmsg[i, 0:32].astype(f32)
    cache_max, cache_sum = cols[:, 32:33], cols[:, 33:34]
    at = chip // 8 * 2
    new_key = jnp.concatenate([kvall[4 * r + at] for r in range(4)], axis=0)
    new_value = jnp.concatenate([kvall[4 * r + at + 1] for r in range(4)], axis=0)
    own = jnp.sum(qown[...].astype(f32) * new_key, axis=1, keepdims=True) * inverse_square_root
    top = jnp.maximum(cache_max, own)
    old_part = jnp.exp(cache_max - top)
    new_part = jnp.exp(own - top)
    denom = cache_sum * old_part + new_part
    return ((cache_out * old_part + new_part * new_value) / denom).astype(bf16)


def kernel(
    hidden_in, w_query, w_keyval, w_out, key_cache, value_cache, key_scale, value_scale, page_counts, slot_pages, trim,
    out_ref,
    hid, wq, wkv, wo, kc, vc, ksv, vsv, cnt, slt, trm,
    part, sib, rsb, qown, kvown, qall, kvall, qs, po, pm, ps, sel, selt, nv, ks0, ks1, vs,
    msg, rmsg, flat, turned, ctx_own, ctx_all, xsend, xrecv,
    load_sem, sib_sem, rs_send, rs_recv, q_send, q_recv, kv_send, kv_recv, o_send, o_recv, c_send, c_recv, x_send, x_recv,
):
    me, col = lax.axis_index("seq"), lax.axis_index("head")
    chip, core = me // 2, lax.rem(me, 2)
    sibling = me + 1 - 2 * core

    barrier = pltpu.get_barrier_semaphore()

    def greet(k):
        pl.semaphore_signal(barrier, inc=1, device_id=(lax.rem(me + k, 32), col), device_id_type=MESH)

    def greet_column(k):
        pl.semaphore_signal(barrier, inc=1, device_id=(me, lax.rem(col + k, 4)), device_id_type=MESH)

    each(1, 32, greet)
    each(1, 4, greet_column)

    def load(k, source, target):
        copy = pltpu.make_async_copy(source, target, load_sem.at[k])
        copy.start()
        return copy

    first = [load(0, hidden_in, hid), load(1, w_query, wq), load(2, w_keyval, wkv)]
    small = [
        load(3, page_counts, cnt), load(4, slot_pages, slt), load(5, trim, trm),
        load(6, key_scale, ksv), load(7, value_scale, vsv),
    ]
    for copy in first:
        copy.wait()
    keys, values, outs = load(8, key_cache, kc), load(9, value_cache, vc), load(10, w_out, wo)
    project(hid, wq, wkv, part)

    def send(source, target, send_sem, recv_sem, device):
        return pltpu.make_async_remote_copy(
            source, target, send_sem, recv_sem, device_id=device, device_id_type=MESH
        )

    pl.semaphore_wait(barrier, 34)
    swap = send(part.at[1 - core], sib, sib_sem.at[0], sib_sem.at[1], (sibling, col))
    swap.start()
    for copy in small:
        copy.wait()
    page_table(cnt, slt, trm, ksv, vsv, sel, selt, nv, ks0, ks1, vs)
    swap.wait()
    sib[...] += part[core]

    def reduce_copy(k, there):
        peer = lax.rem(chip + k, 16)
        return send(sib.at[peer], rsb.at[peer if there else chip], rs_send.at[k], rs_recv.at[peer if there else chip],
                    (2 * peer + core, col))

    each(1, 16, lambda k: reduce_copy(k, False).start())
    rsb[chip] = sib[chip]
    each(1, 16, lambda k: reduce_copy(k, True).wait_recv())
    total = rsb[0]
    for i in range(1, 16):
        total = total + rsb[i]
    qown[...] = total[0:32].astype(bf16)
    kvown[...] = total[32:40].astype(bf16).astype(f32)

    def query_copy(k, there):
        peer = lax.rem(me + k, 32)
        at = peer if there else me
        return send(qown, qall.at[at], q_send.at[k], q_recv.at[at], (peer, col))

    def keyval_copy(k, there):
        peer = lax.rem(chip + k, 16)
        at = peer if there else chip
        return send(kvown, kvall.at[at], kv_send.at[k], kv_recv.at[at], (2 * peer + core, col))

    each(1, 32, lambda k: query_copy(k, False).start())
    each(1, 16, lambda k: keyval_copy(k, False).start())
    qall[me] = qown[...]
    kvall[chip] = kvown[...]
    keys.wait()
    values.wait()
    each(1, 32, lambda k: query_copy(k, True).wait_recv())
    select_query(qall, sel, qs)

    def slots(k):
        attend([k * 32 + u for u in range(32)], kc, vc, qs, nv, ks0, ks1, po, pm, ps)

    each(0, 4, slots)
    for h in range(16):
        fold(h, sel, selt, vs, po, pm, ps, msg)

    def out_copy(k, there):
        peer = lax.rem(me + k, 32)
        at = peer if there else me
        return send(msg.at[peer], rmsg.at[at], o_send.at[k], o_recv.at[at], (peer, col))

    each(1, 32, lambda k: out_copy(k, False).start())
    rmsg[me] = msg[me]
    each(1, 16, lambda k: keyval_copy(k, True).wait_recv())
    each(1, 32, lambda k: out_copy(k, True).wait_recv())
    ctx_own[...] = finish(chip, core, rmsg, qown, kvall, flat, turned)

    def context_copy(k, there):
        peer = lax.rem(me + k, 32)
        at = peer if there else me
        return send(ctx_own, ctx_all.at[at], c_send.at[k], c_recv.at[at], (peer, col))

    each(1, 32, lambda k: context_copy(k, False).start())
    ctx_all[me] = ctx_own[...]
    outs.wait()
    each(1, 32, lambda k: context_copy(k, True).wait_recv())
    context = jnp.concatenate([ctx_all[2 * h : 2 * h + 2].reshape(64, HD) for h in range(16)], axis=1)
    result = jnp.dot(context, wo[...], preferred_element_type=f32)
    xsend[...] = result.astype(bf16)

    def head_copy(k, there):
        peer = lax.rem(col + k, 4)
        at = peer if there else col
        return send(xsend, xrecv.at[at], x_send.at[k], x_recv.at[at], (me, peer))

    each(1, 4, lambda k: head_copy(k, False).start())
    each(1, 4, lambda k: head_copy(k, True).wait_recv())
    for k in range(1, 4):
        result = result + xrecv[lax.rem(col + k, 4)].astype(f32)
    out_ref[...] = result.astype(bf16)

    each(1, 16, lambda k: reduce_copy(k, True).wait_send())
    each(1, 16, lambda k: keyval_copy(k, True).wait_send())
    each(1, 32, lambda k: query_copy(k, True).wait_send())
    each(1, 32, lambda k: out_copy(k, True).wait_send())
    each(1, 32, lambda k: context_copy(k, True).wait_send())
    each(1, 4, lambda k: head_copy(k, True).wait_send())


def body(
    hidden_in, w_query, w_keyval, w_out, key_cache, value_cache, key_scale, value_scale, page_counts, slot_pages, trim
):
    vmem = pltpu.VMEM
    dma = pltpu.SemaphoreType.DMA
    return pl.pallas_call(
        kernel,
        out_shape=jax.ShapeDtypeStruct((64, 256), bf16),
        in_specs=[pl.BlockSpec(memory_space=pltpu.HBM)] * 11,
        out_specs=pl.BlockSpec(memory_space=pltpu.VMEM),
        scratch_shapes=[
            vmem((64, 256), bf16), vmem((256, 2048), bf16), vmem((256, 512), bf16), vmem((2048, 256), bf16),
            vmem((128, PAGE, 256), bf16), vmem((128, PAGE, 256), bf16), vmem((2, 128), f32), vmem((2, 128), f32),
            vmem((1, 64), jnp.int32), vmem((1, 128), jnp.int32), vmem((1, 64), jnp.int32),
            vmem((2, 16, 40, HD), f32), vmem((16, 40, HD), f32), vmem((16, 40, HD), f32),
            vmem((32, HD), bf16), vmem((8, HD), f32), vmem((32, 32, HD), bf16), vmem((16, 8, HD), f32),
            vmem((2048, HD), f32), vmem((2048, HD), f32), vmem((2048, HD), f32), vmem((2048, HD), f32),
            vmem((128, 128), f32), vmem((64, 128), bf16), vmem((128, 128), f32),
            vmem((128, 128), f32), vmem((128, 128), f32), vmem((2, 128, 128), f32),
            vmem((32, 48, HD), bf16), vmem((32, 48, HD), bf16), vmem((128, 128), f32), vmem((128, 128), f32),
            vmem((32, HD), bf16), vmem((32, 32, HD), bf16), vmem((64, 256), bf16), vmem((4, 64, 256), bf16),
            dma((11,)), dma((2,)), dma((16,)), dma((16,)), dma((32,)), dma((32,)), dma((16,)), dma((16,)),
            dma((32,)), dma((32,)), dma((32,)), dma((32,)), dma((4,)), dma((4,)),
        ],
        compiler_params=pltpu.CompilerParams(collective_id=0, has_side_effects=True, vmem_limit_bytes=63 << 20),
        cost_estimate=pl.CostEstimate(flops=300_000_000, bytes_accessed=20_000_000, transcendentals=300_000),
    )(
        hidden_in, w_query, w_keyval, w_out, key_cache, value_cache, key_scale.T, value_scale.T,
        page_counts.reshape(1, 64), slot_pages.reshape(1, 128), trim.reshape(1, 64),
    )


def solution(mesh):
    return jax.shard_map(
        body,
        mesh=mesh,
        in_specs=(
            P(None, "seq"),
            P("seq", "head"),
            P("seq", "head"),
            P("head", "seq"),
            P("seq", None, "head"),
            P("seq", None, "head"),
            P("seq", "head"),
            P("seq", "head"),
            P(),
            P("seq"),
            P(),
        ),
        out_specs=P(None, "seq"),
        check_vma=False,
    )
```

```python
import functools
import math

import jax
import jax.numpy as jnp
from jax import lax
from jax.experimental import pallas as pl
from jax.experimental.pallas import tpu as pltpu
from jax.sharding import PartitionSpec as P

HD = 128
PAGE = 128
MESH = pl.DeviceIdType.MESH
masked_low = -1e30
f32 = jnp.float32
bf16 = jnp.bfloat16
inverse_square_root = 1.0 / math.sqrt(HD)


distance = (0, 1, 2, 1)
AROUND = sorted(
    ((z, y) for z in range(4) for y in range(4) if (z, y) != (0, 0)), key=lambda step: -distance[step[0]] - distance[step[1]]
)
COLUMN = (2, 1, 3)


def step_by(chip, step, back=False):
    z, y = ((4 - step[0]) % 4, (4 - step[1]) % 4) if back else step
    return lax.rem(chip // 4 + z, 4) * 4 + lax.rem(lax.rem(chip, 4) + y, 4)


def project(hid, wq, wkv, part, part_kv):
    x = hid[...]
    for h in range(0, 16, 2):
        y = jnp.dot(x, wq[:, h * HD : (h + 2) * HD], preferred_element_type=f32)
        for c in range(2):
            for j in range(2):
                part[c, h + j] = y[32 * c : 32 * c + 32, HD * j : HD * j + HD]
    for b in range(0, 4, 2):
        y = jnp.dot(x, wkv[:, b * HD : (b + 2) * HD], preferred_element_type=f32)
        for c in range(2):
            for j in range(2):
                for rows in range(4):
                    at = 32 * c + 8 * rows
                    part_kv[c, rows * 4 + b + j] = y[at : at + 8, HD * j : HD * j + HD]


def each(low, high, step):
    def run(k, carry):
        step(k)
        return carry

    lax.fori_loop(low, high, run, 0)


def iota(shape, axis):
    return lax.broadcasted_iota(jnp.int32, shape, axis)


def page_table(cnt, slt, trm, ksv, vsv, sel, selt, nv, ks0, ks1, vs):
    zeros = jnp.zeros((1, 64), f32)
    count = jnp.concatenate([cnt[...].astype(f32), zeros], axis=1)
    trim = jnp.concatenate([trm[...].astype(f32), zeros], axis=1)
    i, j = iota((128, 128), 0), iota((128, 128), 1)
    count_col = jnp.sum(jnp.where(i == j, count, 0.0), axis=1, keepdims=True)
    end_col = jnp.sum(jnp.where(j <= i, count, 0.0), axis=1, keepdims=True)
    end = jnp.sum(jnp.where(i <= j, count_col, 0.0), axis=0, keepdims=True)
    start, start_col = end - count, end_col - count_col
    page = slt[...].astype(f32)

    def column(row):
        return jnp.sum(jnp.where(i == j, row, 0.0), axis=1, keepdims=True)

    page_col = column(page)
    mine = (start <= page_col) & (page_col < end)
    sel[...] = jnp.where(mine, 1.0, 0.0)
    selt[...] = jnp.where((start_col <= page) & (page < end_col), 1.0, 0.0)[:64].astype(bf16)
    left = PAGE * count - trim - PAGE * (page_col - start)
    valid = jnp.sum(jnp.where(mine, left, 0.0), axis=1, keepdims=True)
    nv[...] = jnp.broadcast_to(valid, (128, 128))
    ks0[...] = jnp.broadcast_to(column(ksv[0:1, :]) * inverse_square_root, (128, 128))
    ks1[...] = jnp.broadcast_to(column(ksv[1:2, :]) * inverse_square_root, (128, 128))
    for g in range(2):
        vs[g] = jnp.broadcast_to(column(vsv[g : g + 1, :]), (128, 128))


def select_query(h, qall, sel, qs):
    q = qall[pl.ds(2 * h, 2)].reshape(64, HD)
    at = pl.ds(pl.multiple_of(h * 128, 128), 128)
    qs[at, :] = jnp.dot(sel[:, 0:64].astype(bf16), q, preferred_element_type=f32)


def attend(slots, kc, vc, qs, nv, ks0, ks1, po, pm, ps):
    none = jnp.zeros((8, HD), f32)
    token = iota((16, PAGE), 1).astype(f32)
    scores, valids = [], []
    for slot in slots:
        q = qs[pl.ds(slot, 16, stride=128), :]
        left = jnp.concatenate([q[0:8], none], axis=0).astype(bf16)
        right = jnp.concatenate([none, q[8:16]], axis=0).astype(bf16)
        query = jnp.concatenate([left, right], axis=1)
        score = lax.dot_general(query, kc[slot], (((1,), (1,)), ((), ())), preferred_element_type=f32)
        scale0 = jnp.broadcast_to(ks0[pl.ds(slot, 1), :], (8, PAGE))
        scale1 = jnp.broadcast_to(ks1[pl.ds(slot, 1), :], (8, PAGE))
        score = score * jnp.concatenate([scale0, scale1], axis=0)
        valid = token < jnp.broadcast_to(nv[pl.ds(slot, 1), :], (16, PAGE))
        scores.append(jnp.where(valid, score, masked_low))
        valids.append(valid)
    tops = [jnp.max(score, axis=1, keepdims=True) for score in scores]
    probs = [
        jnp.where(valid, jnp.exp(score - top), 0.0).astype(bf16)
        for score, valid, top in zip(scores, valids, tops)
    ]
    totals = [jnp.sum(prob.astype(f32), axis=1, keepdims=True) for prob in probs]
    outs = [jnp.dot(prob, vc[slot], preferred_element_type=f32) for slot, prob in zip(slots, probs)]
    for slot, out, top, total in zip(slots, outs, tops, totals):
        at = pl.ds(pl.multiple_of(slot * 16, 16), 16)
        po[at, :] = jnp.concatenate([out[0:8, 0:HD], out[8:16, HD : 2 * HD]], axis=0)
        pm[at, :] = jnp.broadcast_to(top, (16, HD))
        ps[at, :] = jnp.broadcast_to(total, (16, HD))


def fold(h, sel, selt, vs, po, pm, ps, msg, stats):
    rows = pl.ds(h, 128, stride=16)
    mine = sel[...] > 0.5
    page_max = pm[rows, :]
    dev_max = jnp.max(jnp.where(mine, page_max, masked_low), axis=0, keepdims=True)
    slot_max = jnp.max(jnp.where(mine, dev_max, masked_low), axis=1, keepdims=True)
    weight = jnp.exp(page_max - slot_max)
    dev_sum = jnp.sum(jnp.where(mine, ps[rows, :] * weight, 0.0), axis=0, keepdims=True)
    stats[h] = jnp.concatenate([dev_max[:, 0:64], dev_sum[:, 0:64]], axis=1)
    weighted = (po[rows, :] * (weight * vs[h // 8])).astype(bf16)
    dev_out = jnp.dot(selt[...], weighted, preferred_element_type=f32).astype(bf16)
    for c in range(2):
        msg[2 * h + c] = dev_out[32 * c : 32 * c + 32]


def own_score(chip, qown, kvall):
    at = chip // 8 * 2
    new_key = jnp.concatenate([kvall[4 * r + at] for r in range(4)], axis=0)
    new_value = jnp.concatenate([kvall[4 * r + at + 1] for r in range(4)], axis=0)
    own = jnp.sum(qown[...].astype(f32) * new_key, axis=1, keepdims=True) * inverse_square_root
    return own, new_value


def finish(core, rmsg, rstats, own, new_value, flat, turned):
    stats = rstats[...].reshape(32, 128)
    cache_max = jnp.max(stats, axis=0, keepdims=True)
    factors = jnp.exp(stats - cache_max)
    sums = jnp.concatenate([stats[:, 64:128], stats[:, 0:64]], axis=1)
    flat[...] = jnp.zeros((128, 128), f32)
    flat[0:32] = factors
    flat[32:33] = cache_max
    flat[33:34] = jnp.sum(sums * factors, axis=0, keepdims=True)
    turned[...] = flat[...].T
    cols = turned[pl.ds(pl.multiple_of(core * 32, 32), 32), :]
    cache_out = jnp.zeros((32, HD), f32)
    for i in range(32):
        cache_out = cache_out + cols[:, i : i + 1] * rmsg[i].astype(f32)
    cache_max, cache_sum = cols[:, 32:33], cols[:, 33:34]
    top = jnp.maximum(cache_max, own)
    old_part = jnp.exp(cache_max - top)
    new_part = jnp.exp(own - top)
    denom = cache_sum * old_part + new_part
    return ((cache_out * old_part + new_part * new_value) / denom).astype(bf16)


def kernel(
    hidden_in, w_query, w_keyval, w_out, key_cache, value_cache, key_scale, value_scale, page_counts, slot_pages, trim,
    out_ref,
    hid, wq, wkv, wo, kc, vc, ksv, vsv, cnt, slt, trm,
    part, sib, rsb, part_kv, sib_kv, rsb_kv, qown, kvown, qall, kvall, qs, po, pm, ps, sel, selt, nv, ks0, ks1, vs,
    msg, rmsg, stats, rstats, flat, turned, ctx_own, ctx_all, xsend, xrecv,
    load_sem, sib_sem, rs_send, rs_recv, rk_send, rk_recv, q_send, q_recv, kv_send, kv_recv,
    o_send, o_recv, s_send, s_recv, c_send, c_recv, x_send, x_recv,
):
    me, col = lax.axis_index("seq"), lax.axis_index("head")
    chip, core = me // 2, lax.rem(me, 2)
    other = 1 - core
    sibling = 2 * chip + other

    def load(k, source, target):
        copy = pltpu.make_async_copy(source, target, load_sem.at[k])
        copy.start()
        return copy

    first = [load(0, hidden_in, hid), load(1, w_query, wq), load(2, w_keyval, wkv)]

    barrier = pltpu.get_barrier_semaphore()

    def greet(seq, head):
        pl.semaphore_signal(barrier, inc=1, device_id=(seq, head), device_id_type=MESH)

    for step in AROUND:
        for c in range(2):
            greet(2 * step_by(chip, step) + c, col)
    for k in COLUMN:
        for c in range(2):
            greet(2 * chip + c, lax.rem(col + k, 4))
    greet(sibling, col)

    small = [
        load(3, page_counts, cnt), load(4, slot_pages, slt), load(5, trim, trm),
        load(6, key_scale, ksv), load(7, value_scale, vsv),
    ]
    for copy in first:
        copy.wait()
    keys, values, outs = load(8, key_cache, kc), load(9, value_cache, vc), load(10, w_out, wo.at[core])
    project(hid, wq, wkv, part, part_kv)

    def send(source, target, send_sem, recv_sem, seq, head=col):
        return pltpu.make_async_remote_copy(
            source, target, send_sem, recv_sem, device_id=(seq, head), device_id_type=MESH
        )

    pl.semaphore_wait(barrier, 37)
    swap = send(part.at[other], sib, sib_sem.at[0], sib_sem.at[1], sibling)
    swap_kv = send(part_kv.at[other], sib_kv, sib_sem.at[2], sib_sem.at[3], sibling)
    swap.start()
    swap_kv.start()
    for copy in small:
        copy.wait()
    page_table(cnt, slt, trm, ksv, vsv, sel, selt, nv, ks0, ks1, vs)
    swap.wait_recv()
    sib[...] += part[core]

    reduces = []
    for i, step in enumerate(AROUND):
        peer = step_by(chip, step)
        reduces.append(send(sib.at[peer], rsb.at[i], rs_send.at[i], rs_recv.at[i], 2 * peer + core))
        reduces[-1].start()
    swap_kv.wait_recv()
    sib_kv[...] += part_kv[core]
    reduces_kv = []
    for i, step in enumerate(AROUND):
        peer = step_by(chip, step)
        reduces_kv.append(send(sib_kv.at[peer], rsb_kv.at[i], rk_send.at[i], rk_recv.at[i], 2 * peer + core))
        reduces_kv[-1].start()
    total = sib[chip]
    for i in reversed(range(15)):
        reduces[i].wait_recv()
        total = total + rsb[i]
    qown[...] = total.astype(bf16)

    queries = []
    for i, step in enumerate(AROUND):
        for c in range(2):
            peer = 2 * step_by(chip, step) + (other if c else core)
            queries.append(send(qown, qall.at[me], q_send.at[2 * i + c], q_recv.at[2 * i + c], peer))
            queries[-1].start()
    queries.append(send(qown, qall.at[me], q_send.at[30], q_recv.at[30], sibling))
    queries[-1].start()
    qall[me] = qown[...]

    total = sib_kv[chip]
    for i in reversed(range(15)):
        reduces_kv[i].wait_recv()
        total = total + rsb_kv[i]
    kvown[...] = total.astype(bf16).astype(f32)
    keyvals = []
    for i, step in enumerate(AROUND):
        peer = 2 * step_by(chip, step) + core
        keyvals.append(send(kvown, kvall.at[chip], kv_send.at[i], kv_recv.at[i], peer))
        keyvals[-1].start()
    kvall[chip] = kvown[...]
    outs.wait()
    share = send(wo.at[core], wo.at[core], sib_sem.at[4], sib_sem.at[5], sibling)
    share.start()

    def query_from(i, c, source):
        return send(qown, qall.at[source], q_send.at[2 * i + c], q_recv.at[2 * i + c], source)

    query_from(15, 0, sibling).wait_recv()
    select_query(chip, qall, sel, qs)
    for i in reversed(range(15)):
        source = step_by(chip, AROUND[i], back=True)
        for c in range(2):
            query_from(i, c, 2 * source + (other if c else core)).wait_recv()
        select_query(source, qall, sel, qs)
    keys.wait()
    values.wait()

    def slots(k):
        attend([k * 32 + u for u in range(32)], kc, vc, qs, nv, ks0, ks1, po, pm, ps)

    each(0, 4, slots)

    sent = []
    for i in range(0, 15, 4):
        group = range(i, min(i + 4, 15))
        heads = {k: step_by(chip, AROUND[k]) for k in group}
        for k in group:
            fold(heads[k], sel, selt, vs, po, pm, ps, msg, stats)
        for k in group:
            for c in range(2):
                half = other if c else core
                at = 2 * k + c
                peer = 2 * heads[k] + half
                sent.append(send(msg.at[peer], rmsg.at[at], o_send.at[at], o_recv.at[at], peer))
                sent.append(send(stats.at[heads[k]], rstats.at[at], s_send.at[at], s_recv.at[at], peer))
                sent[-2].start()
                sent[-1].start()
    fold(chip, sel, selt, vs, po, pm, ps, msg, stats)
    sent.append(send(msg.at[sibling], rmsg.at[30], o_send.at[30], o_recv.at[30], sibling))
    sent.append(send(stats.at[chip], rstats.at[30], s_send.at[30], s_recv.at[30], sibling))
    sent[-2].start()
    sent[-1].start()
    rmsg[31] = msg[me]
    rstats[31] = stats[chip]
    for i in reversed(range(15)):
        source = step_by(chip, AROUND[i], back=True)
        send(kvown, kvall.at[source], kv_send.at[i], kv_recv.at[i], 2 * source + core).wait_recv()
    own, new_value = own_score(chip, qown, kvall)
    for copy in reversed(sent):
        copy.wait_recv()
    ctx_own[...] = finish(core, rmsg, rstats, own, new_value, flat, turned)

    contexts = []
    for i, step in enumerate(AROUND):
        peer = 2 * step_by(chip, step) + core
        contexts.append(send(ctx_own, ctx_all.at[chip], c_send.at[i], c_recv.at[i], peer))
        contexts[-1].start()
    share.wait_send()
    send(wo.at[core], wo.at[other], sib_sem.at[4], sib_sem.at[5], sibling).wait_recv()

    def project_out(h, context, result):
        rows = pl.ds(pl.multiple_of(h * HD, HD), HD)
        return [y + jnp.dot(context, wo[c, rows, :], preferred_element_type=f32) for c, y in enumerate(result)]

    result = project_out(chip, ctx_own[...], [jnp.zeros((32, 256), f32)] * 2)
    for i in reversed(range(15)):
        source = step_by(chip, AROUND[i], back=True)
        send(ctx_own, ctx_all.at[source], c_send.at[i], c_recv.at[i], 2 * source + core).wait_recv()
        result = project_out(source, ctx_all[source], result)
    for c in range(2):
        xsend[c] = result[c].astype(bf16)

    ends = []
    for k in COLUMN:
        for c in range(2):
            half = other if c else core
            at = 2 * k + c
            there = lax.rem(col + k, 4)
            ends.append(send(xsend.at[half], xrecv.at[core, col], x_send.at[at], x_recv.at[at], 2 * chip + half, there))
            ends[-1].start()
    ends.append(send(xsend.at[other], xrecv.at[core, col], x_send.at[1], x_recv.at[1], sibling))
    ends[-1].start()
    xrecv[core, col] = xsend[core]
    for k in range(4):
        source = lax.rem(col + 4 - k, 4)
        for c in range(2):
            if k or c:
                half = other if c else core
                at = 2 * k + c
                send(xsend.at[0], xrecv.at[half, source], x_send.at[at], x_recv.at[at], 2 * chip + half, source).wait_recv()
    for c in range(2):
        result = xrecv[c, 0].astype(f32)
        for k in range(1, 4):
            result = result + xrecv[c, k].astype(f32)
        out_ref[32 * c : 32 * c + 32] = result.astype(bf16)

    swap.wait_send()
    swap_kv.wait_send()
    for copy in reduces + reduces_kv + queries + keyvals + sent + contexts + ends:
        copy.wait_send()


def body(
    hidden_in, w_query, w_keyval, w_out, key_cache, value_cache, key_scale, value_scale, page_counts, slot_pages, trim
):
    vmem = pltpu.VMEM
    dma = pltpu.SemaphoreType.DMA
    return pl.pallas_call(
        kernel,
        out_shape=jax.ShapeDtypeStruct((64, 256), bf16),
        in_specs=[pl.BlockSpec(memory_space=pltpu.HBM)] * 11,
        out_specs=pl.BlockSpec(memory_space=pltpu.VMEM),
        scratch_shapes=[
            vmem((64, 256), bf16), vmem((256, 2048), bf16), vmem((256, 512), bf16), vmem((2, 2048, 256), bf16),
            vmem((128, PAGE, 256), bf16), vmem((128, PAGE, 256), bf16), vmem((2, 128), f32), vmem((2, 128), f32),
            vmem((1, 64), jnp.int32), vmem((1, 128), jnp.int32), vmem((1, 64), jnp.int32),
            vmem((2, 16, 32, HD), f32), vmem((16, 32, HD), f32), vmem((15, 32, HD), f32),
            vmem((2, 16, 8, HD), f32), vmem((16, 8, HD), f32), vmem((15, 8, HD), f32),
            vmem((32, HD), bf16), vmem((8, HD), f32), vmem((32, 32, HD), bf16), vmem((16, 8, HD), f32),
            vmem((2048, HD), f32), vmem((2048, HD), f32), vmem((2048, HD), f32), vmem((2048, HD), f32),
            vmem((128, 128), f32), vmem((64, 128), bf16), vmem((128, 128), f32),
            vmem((128, 128), f32), vmem((128, 128), f32), vmem((2, 128, 128), f32),
            vmem((32, 32, HD), bf16), vmem((32, 32, HD), bf16), vmem((16, 1, 128), f32), vmem((32, 1, 128), f32),
            vmem((128, 128), f32), vmem((128, 128), f32),
            vmem((32, HD), bf16), vmem((16, 32, HD), bf16), vmem((2, 32, 256), bf16), vmem((2, 4, 32, 256), bf16),
            dma((11,)), dma((6,)), dma((15,)), dma((15,)), dma((15,)), dma((15,)), dma((31,)), dma((31,)),
            dma((15,)), dma((15,)), dma((31,)), dma((31,)), dma((31,)), dma((31,)), dma((15,)), dma((15,)),
            dma((8,)), dma((8,)),
        ],
        compiler_params=pltpu.CompilerParams(collective_id=0, has_side_effects=True, vmem_limit_bytes=63 << 20),
        cost_estimate=pl.CostEstimate(flops=300_000_000, bytes_accessed=20_000_000, transcendentals=300_000),
    )(
        hidden_in, w_query, w_keyval, w_out, key_cache, value_cache, key_scale.T, value_scale.T,
        page_counts.reshape(1, 64), slot_pages.reshape(1, 128), trim.reshape(1, 64),
    )


def solution(mesh):
    return jax.shard_map(
        body,
        mesh=mesh,
        in_specs=(
            P(None, "seq"),
            P("seq", "head"),
            P("seq", "head"),
            P("head", "seq"),
            P("seq", None, "head"),
            P("seq", None, "head"),
            P("seq", "head"),
            P("seq", "head"),
            P(),
            P("seq"),
            P(),
        ),
        out_specs=P(None, "seq"),
        check_vma=False,
    )
```

```python
import functools
import math

import jax
import jax.numpy as jnp
from jax import lax
from jax.experimental import pallas as pl
from jax.experimental.pallas import tpu as pltpu
from jax.sharding import PartitionSpec as P

HD = 128
PAGE = 128
MESH = pl.DeviceIdType.MESH
masked_low = -1e30
f32 = jnp.float32
bf16 = jnp.bfloat16
inverse_square_root = 1.0 / math.sqrt(HD)


distance = (0, 1, 2, 1)
AROUND = sorted(
    ((z, y) for z in range(4) for y in range(4) if (z, y) != (0, 0)), key=lambda step: -distance[step[0]] - distance[step[1]]
)
COLUMN = (2, 1, 3)
GROUPS = (range(0, 5), range(5, 11), range(11, 15))
GROUP = [g for g, chips in enumerate(GROUPS) for _ in chips]


def step_by(chip, step, back=False):
    z, y = ((4 - step[0]) % 4, (4 - step[1]) % 4) if back else step
    return lax.rem(chip // 4 + z, 4) * 4 + lax.rem(lax.rem(chip, 4) + y, 4)


def project(hid, wq, wkv, part, part_kv):
    x = hid[...]
    for h in range(0, 16, 2):
        y = jnp.dot(x, wq[:, h * HD : (h + 2) * HD], preferred_element_type=f32)
        for c in range(2):
            for j in range(2):
                part[c, h + j] = y[32 * c : 32 * c + 32, HD * j : HD * j + HD]
    for b in range(0, 4, 2):
        y = jnp.dot(x, wkv[:, b * HD : (b + 2) * HD], preferred_element_type=f32)
        for c in range(2):
            for j in range(2):
                for rows in range(4):
                    at = 32 * c + 8 * rows
                    part_kv[c, rows * 4 + b + j] = y[at : at + 8, HD * j : HD * j + HD]


def each(low, high, step):
    def run(k, carry):
        step(k)
        return carry

    lax.fori_loop(low, high, run, 0)


def iota(shape, axis):
    return lax.broadcasted_iota(jnp.int32, shape, axis)


def page_table(cnt, slt, trm, ksv, vsv, sel, selt, nv, ks0, ks1, vs):
    zeros = jnp.zeros((1, 64), f32)
    count = jnp.concatenate([cnt[...].astype(f32), zeros], axis=1)
    trim = jnp.concatenate([trm[...].astype(f32), zeros], axis=1)
    i, j = iota((128, 128), 0), iota((128, 128), 1)
    count_col = jnp.sum(jnp.where(i == j, count, 0.0), axis=1, keepdims=True)
    end_col = jnp.sum(jnp.where(j <= i, count, 0.0), axis=1, keepdims=True)
    end = jnp.sum(jnp.where(i <= j, count_col, 0.0), axis=0, keepdims=True)
    start, start_col = end - count, end_col - count_col
    page = slt[...].astype(f32)

    def column(row):
        return jnp.sum(jnp.where(i == j, row, 0.0), axis=1, keepdims=True)

    page_col = column(page)
    mine = (start <= page_col) & (page_col < end)
    sel[...] = jnp.where(mine, 1.0, 0.0)
    selt[...] = jnp.where((start_col <= page) & (page < end_col), 1.0, 0.0)[:64].astype(bf16)
    left = PAGE * count - trim - PAGE * (page_col - start)
    valid = jnp.sum(jnp.where(mine, left, 0.0), axis=1, keepdims=True)
    nv[...] = jnp.broadcast_to(valid, (128, 128))
    ks0[...] = jnp.broadcast_to(column(ksv[0:1, :]) * inverse_square_root, (128, 128))
    ks1[...] = jnp.broadcast_to(column(ksv[1:2, :]) * inverse_square_root, (128, 128))
    for g in range(2):
        vs[g] = jnp.broadcast_to(column(vsv[g : g + 1, :]), (128, 128))


def select_query(h, qall, sel, qs):
    q = qall[pl.ds(2 * h, 2)].reshape(64, HD)
    at = pl.ds(pl.multiple_of(h * 128, 128), 128)
    qs[at, :] = jnp.dot(sel[:, 0:64].astype(bf16), q, preferred_element_type=f32)


def attend(slots, kc, vc, qs, nv, ks0, ks1, po, pm, ps):
    none = jnp.zeros((8, HD), f32)
    token = iota((16, PAGE), 1).astype(f32)
    scores, valids = [], []
    for slot in slots:
        q = qs[pl.ds(slot, 16, stride=128), :]
        left = jnp.concatenate([q[0:8], none], axis=0).astype(bf16)
        right = jnp.concatenate([none, q[8:16]], axis=0).astype(bf16)
        query = jnp.concatenate([left, right], axis=1)
        score = lax.dot_general(query, kc[slot], (((1,), (1,)), ((), ())), preferred_element_type=f32)
        scale0 = jnp.broadcast_to(ks0[pl.ds(slot, 1), :], (8, PAGE))
        scale1 = jnp.broadcast_to(ks1[pl.ds(slot, 1), :], (8, PAGE))
        score = score * jnp.concatenate([scale0, scale1], axis=0)
        valid = token < jnp.broadcast_to(nv[pl.ds(slot, 1), :], (16, PAGE))
        scores.append(jnp.where(valid, score, masked_low))
        valids.append(valid)
    tops = [jnp.max(score, axis=1, keepdims=True) for score in scores]
    probs = [
        jnp.where(valid, jnp.exp(score - top), 0.0).astype(bf16)
        for score, valid, top in zip(scores, valids, tops)
    ]
    totals = [jnp.sum(prob.astype(f32), axis=1, keepdims=True) for prob in probs]
    outs = [jnp.dot(prob, vc[slot], preferred_element_type=f32) for slot, prob in zip(slots, probs)]
    for slot, out, top, total in zip(slots, outs, tops, totals):
        at = pl.ds(pl.multiple_of(slot * 16, 16), 16)
        po[at, :] = jnp.concatenate([out[0:8, 0:HD], out[8:16, HD : 2 * HD]], axis=0)
        pm[at, :] = jnp.broadcast_to(top, (16, HD))
        ps[at, :] = jnp.broadcast_to(total, (16, HD))


def fold(h, sel, selt, vs, po, pm, ps, msg, stats):
    rows = pl.ds(h, 128, stride=16)
    mine = sel[...] > 0.5
    page_max = pm[rows, :]
    dev_max = jnp.max(jnp.where(mine, page_max, masked_low), axis=0, keepdims=True)
    slot_max = jnp.max(jnp.where(mine, dev_max, masked_low), axis=1, keepdims=True)
    weight = jnp.exp(page_max - slot_max)
    dev_sum = jnp.sum(jnp.where(mine, ps[rows, :] * weight, 0.0), axis=0, keepdims=True)
    stats[h] = jnp.concatenate([dev_max[:, 0:64], dev_sum[:, 0:64]], axis=1)
    weighted = (po[rows, :] * (weight * vs[h // 8])).astype(bf16)
    dev_out = jnp.dot(selt[...], weighted, preferred_element_type=f32).astype(bf16)
    for c in range(2):
        msg[2 * h + c] = dev_out[32 * c : 32 * c + 32]


def own_score(chip, qown, kvall):
    at = chip // 8 * 2
    new_key = jnp.concatenate([kvall[4 * r + at] for r in range(4)], axis=0)
    new_value = jnp.concatenate([kvall[4 * r + at + 1] for r in range(4)], axis=0)
    own = jnp.sum(qown[...].astype(f32) * new_key, axis=1, keepdims=True) * inverse_square_root
    return own, new_value


def finish(core, rmsg, rstats, own, new_value, flat, turned):
    stats = rstats[...].reshape(32, 128)
    cache_max = jnp.max(stats, axis=0, keepdims=True)
    factors = jnp.exp(stats - cache_max)
    sums = jnp.concatenate([stats[:, 64:128], stats[:, 0:64]], axis=1)
    flat[...] = jnp.zeros((128, 128), f32)
    flat[0:32] = factors
    flat[32:33] = cache_max
    flat[33:34] = jnp.sum(sums * factors, axis=0, keepdims=True)
    turned[...] = flat[...].T
    cols = turned[pl.ds(pl.multiple_of(core * 32, 32), 32), :]
    cache_out = jnp.zeros((32, HD), f32)
    for i in range(32):
        cache_out = cache_out + cols[:, i : i + 1] * rmsg[i].astype(f32)
    cache_max, cache_sum = cols[:, 32:33], cols[:, 33:34]
    top = jnp.maximum(cache_max, own)
    old_part = jnp.exp(cache_max - top)
    new_part = jnp.exp(own - top)
    denom = cache_sum * old_part + new_part
    return ((cache_out * old_part + new_part * new_value) / denom).astype(bf16)


def kernel(
    hidden_in, w_query, w_keyval, w_out, key_cache, value_cache, key_scale, value_scale, page_counts, slot_pages, trim,
    out_ref,
    hid, wq, wkv, wo, kc, vc, ksv, vsv, cnt, slt, trm,
    part, sib, rsb, part_kv, sib_kv, rsb_kv, qown, kvown, qall, kvall, qs, po, pm, ps, sel, selt, nv, ks0, ks1, vs,
    msg, rmsg, stats, rstats, flat, turned, ctx_own, ctx_all, xsend, xrecv,
    load_sem, sib_sem, send_sem, rs_recv, q_recv, kv_recv, o_recv, c_recv, x_recv,
):
    me, col = lax.axis_index("seq"), lax.axis_index("head")
    chip, core = me // 2, lax.rem(me, 2)
    other = 1 - core
    sibling = 2 * chip + other

    def load(k, source, target):
        copy = pltpu.make_async_copy(source, target, load_sem.at[k])
        copy.start()
        return copy

    first = [load(0, hidden_in, hid), load(1, w_query, wq), load(2, w_keyval, wkv)]

    barrier = pltpu.get_barrier_semaphore()

    def greet(seq, head):
        pl.semaphore_signal(barrier, inc=1, device_id=(seq, head), device_id_type=MESH)

    for step in AROUND:
        for c in range(2):
            greet(2 * step_by(chip, step) + c, col)
    for k in COLUMN:
        for c in range(2):
            greet(2 * chip + c, lax.rem(col + k, 4))
    greet(sibling, col)

    small = [
        load(3, page_counts, cnt), load(4, slot_pages, slt), load(5, trim, trm),
        load(6, key_scale, ksv), load(7, value_scale, vsv),
    ]
    for copy in first:
        copy.wait()
    keys, values, outs = load(8, key_cache, kc), load(9, value_cache, vc), load(10, w_out, wo.at[core])
    project(hid, wq, wkv, part, part_kv)

    def send(source, target, send_sem, recv_sem, seq, head=col):
        return pltpu.make_async_remote_copy(
            source, target, send_sem, recv_sem, device_id=(seq, head), device_id_type=MESH
        )

    pl.semaphore_wait(barrier, 37)
    swap = send(part.at[other], sib, sib_sem.at[0], sib_sem.at[1], sibling)
    swap_kv = send(part_kv.at[other], sib_kv, sib_sem.at[2], sib_sem.at[3], sibling)
    swap.start()
    swap_kv.start()
    for copy in small:
        copy.wait()
    page_table(cnt, slt, trm, ksv, vsv, sel, selt, nv, ks0, ks1, vs)
    swap.wait_recv()
    sib[...] += part[core]

    def landed(ref, semaphore):
        send(ref, ref, semaphore, semaphore, sibling).wait_recv()

    def left(ref, semaphore):
        send(ref, ref, semaphore, semaphore, sibling).wait_send()

    for i, step in enumerate(AROUND):
        peer = step_by(chip, step)
        send(sib.at[peer], rsb.at[i], send_sem.at[0], rs_recv.at[GROUP[i]], 2 * peer + core).start()
    swap_kv.wait_recv()
    sib_kv[...] += part_kv[core]
    total = sib[chip]
    for g in (2, 1, 0):
        landed(rsb.at[pl.ds(GROUPS[g][0], len(GROUPS[g]))], rs_recv.at[g])
        for i in GROUPS[g]:
            total = total + rsb[i]
    qown[...] = total.astype(bf16)

    for i, step in enumerate(AROUND):
        for c in range(2):
            peer = 2 * step_by(chip, step) + (other if c else core)
            send(qown, qall.at[me], send_sem.at[1], q_recv.at[GROUP[i]], peer).start()
    send(qown, qall.at[me], send_sem.at[1], q_recv.at[2], sibling).start()
    for i, step in enumerate(AROUND):
        peer = step_by(chip, step)
        send(sib_kv.at[peer], rsb_kv.at[i], send_sem.at[2], kv_recv.at[0], 2 * peer + core).start()
    qall[me] = qown[...]
    outs.wait()
    share = send(wo.at[core], wo.at[core], sib_sem.at[4], sib_sem.at[5], sibling)
    share.start()

    for g in (2, 1, 0):
        landed(qall.at[pl.ds(0, 2 * len(GROUPS[g]) + (g == 2))], q_recv.at[g])
        if g == 2:
            select_query(chip, qall, sel, qs)
        for i in GROUPS[g]:
            select_query(step_by(chip, AROUND[i], back=True), qall, sel, qs)
    landed(rsb_kv, kv_recv.at[0])
    total = sib_kv[chip]
    for i in range(15):
        total = total + rsb_kv[i]
    kvown[...] = total.astype(bf16).astype(f32)
    for i, step in enumerate(AROUND):
        peer = 2 * step_by(chip, step) + core
        send(kvown, kvall.at[chip], send_sem.at[3], kv_recv.at[1], peer).start()
    kvall[chip] = kvown[...]
    keys.wait()
    values.wait()

    def slots(k):
        attend([k * 32 + u for u in range(32)], kc, vc, qs, nv, ks0, ks1, po, pm, ps)

    each(0, 4, slots)

    for i in range(0, 15, 4):
        group = range(i, min(i + 4, 15))
        heads = {k: step_by(chip, AROUND[k]) for k in group}
        for k in group:
            fold(heads[k], sel, selt, vs, po, pm, ps, msg, stats)
        for k in group:
            for c in range(2):
                at = 2 * k + c
                peer = 2 * heads[k] + (other if c else core)
                send(msg.at[peer], rmsg.at[at], send_sem.at[4], o_recv.at[0], peer).start()
                send(stats.at[heads[k]], rstats.at[at], send_sem.at[5], o_recv.at[1], peer).start()
    fold(chip, sel, selt, vs, po, pm, ps, msg, stats)
    send(msg.at[sibling], rmsg.at[30], send_sem.at[4], o_recv.at[0], sibling).start()
    send(stats.at[chip], rstats.at[30], send_sem.at[5], o_recv.at[1], sibling).start()
    rmsg[31] = msg[me]
    rstats[31] = stats[chip]
    landed(kvall.at[pl.ds(0, 15)], kv_recv.at[1])
    own, new_value = own_score(chip, qown, kvall)
    landed(rstats.at[pl.ds(0, 31)], o_recv.at[1])
    landed(rmsg.at[pl.ds(0, 31)], o_recv.at[0])
    ctx_own[...] = finish(core, rmsg, rstats, own, new_value, flat, turned)

    for i, step in enumerate(AROUND):
        peer = 2 * step_by(chip, step) + core
        send(ctx_own, ctx_all.at[chip], send_sem.at[6], c_recv.at[GROUP[i]], peer).start()
    share.wait_send()
    landed(wo.at[other], sib_sem.at[5])

    def project_out(h, context, result):
        rows = pl.ds(pl.multiple_of(h * HD, HD), HD)
        return [y + jnp.dot(context, wo[c, rows, :], preferred_element_type=f32) for c, y in enumerate(result)]

    result = project_out(chip, ctx_own[...], [jnp.zeros((32, 256), f32)] * 2)
    for g in (2, 1, 0):
        landed(ctx_all.at[pl.ds(0, len(GROUPS[g]))], c_recv.at[g])
        for i in GROUPS[g]:
            source = step_by(chip, AROUND[i], back=True)
            result = project_out(source, ctx_all[source], result)
    for c in range(2):
        xsend[c] = result[c].astype(bf16)

    mine = 4 * core + col
    for k in COLUMN:
        for half in (core, other):
            there = lax.rem(col + k, 4)
            send(xsend.at[half], xrecv.at[mine], send_sem.at[7], x_recv.at[0], 2 * chip + half, there).start()
    send(xsend.at[other], xrecv.at[mine], send_sem.at[7], x_recv.at[0], sibling).start()
    xrecv[mine] = xsend[core]
    landed(xrecv.at[pl.ds(0, 7)], x_recv.at[0])
    for c in range(2):
        result = xrecv[4 * c].astype(f32)
        for k in range(1, 4):
            result = result + xrecv[4 * c + k].astype(f32)
        out_ref[32 * c : 32 * c + 32] = result.astype(bf16)

    swap.wait_send()
    swap_kv.wait_send()
    left(rsb, send_sem.at[0])
    left(qall.at[pl.ds(0, 31)], send_sem.at[1])
    left(rsb_kv, send_sem.at[2])
    left(kvall.at[pl.ds(0, 15)], send_sem.at[3])
    left(rmsg.at[pl.ds(0, 31)], send_sem.at[4])
    left(rstats.at[pl.ds(0, 31)], send_sem.at[5])
    left(ctx_all.at[pl.ds(0, 15)], send_sem.at[6])
    left(xrecv.at[pl.ds(0, 7)], send_sem.at[7])


def body(
    hidden_in, w_query, w_keyval, w_out, key_cache, value_cache, key_scale, value_scale, page_counts, slot_pages, trim
):
    vmem = pltpu.VMEM
    dma = pltpu.SemaphoreType.DMA
    return pl.pallas_call(
        kernel,
        out_shape=jax.ShapeDtypeStruct((64, 256), bf16),
        in_specs=[pl.BlockSpec(memory_space=pltpu.HBM)] * 11,
        out_specs=pl.BlockSpec(memory_space=pltpu.VMEM),
        scratch_shapes=[
            vmem((64, 256), bf16), vmem((256, 2048), bf16), vmem((256, 512), bf16), vmem((2, 2048, 256), bf16),
            vmem((128, PAGE, 256), bf16), vmem((128, PAGE, 256), bf16), vmem((2, 128), f32), vmem((2, 128), f32),
            vmem((1, 64), jnp.int32), vmem((1, 128), jnp.int32), vmem((1, 64), jnp.int32),
            vmem((2, 16, 32, HD), f32), vmem((16, 32, HD), f32), vmem((15, 32, HD), f32),
            vmem((2, 16, 8, HD), f32), vmem((16, 8, HD), f32), vmem((15, 8, HD), f32),
            vmem((32, HD), bf16), vmem((8, HD), f32), vmem((32, 32, HD), bf16), vmem((16, 8, HD), f32),
            vmem((2048, HD), f32), vmem((2048, HD), f32), vmem((2048, HD), f32), vmem((2048, HD), f32),
            vmem((128, 128), f32), vmem((64, 128), bf16), vmem((128, 128), f32),
            vmem((128, 128), f32), vmem((128, 128), f32), vmem((2, 128, 128), f32),
            vmem((32, 32, HD), bf16), vmem((32, 32, HD), bf16), vmem((16, 1, 128), f32), vmem((32, 1, 128), f32),
            vmem((128, 128), f32), vmem((128, 128), f32),
            vmem((32, HD), bf16), vmem((16, 32, HD), bf16), vmem((2, 32, 256), bf16), vmem((8, 32, 256), bf16),
            dma((11,)), dma((6,)), dma((8,)), dma((3,)), dma((3,)), dma((2,)), dma((2,)), dma((3,)), dma((1,)),
        ],
        compiler_params=pltpu.CompilerParams(collective_id=0, has_side_effects=True, vmem_limit_bytes=63 << 20),
        cost_estimate=pl.CostEstimate(flops=300_000_000, bytes_accessed=20_000_000, transcendentals=300_000),
    )(
        hidden_in, w_query, w_keyval, w_out, key_cache, value_cache, key_scale.T, value_scale.T,
        page_counts.reshape(1, 64), slot_pages.reshape(1, 128), trim.reshape(1, 64),
    )


def solution(mesh):
    return jax.shard_map(
        body,
        mesh=mesh,
        in_specs=(
            P(None, "seq"),
            P("seq", "head"),
            P("seq", "head"),
            P("head", "seq"),
            P("seq", None, "head"),
            P("seq", None, "head"),
            P("seq", "head"),
            P("seq", "head"),
            P(),
            P("seq"),
            P(),
        ),
        out_specs=P(None, "seq"),
        check_vma=False,
    )
```

```python
import functools
import math

import jax
import jax.numpy as jnp
from jax import lax
from jax.experimental import pallas as pl
from jax.experimental.pallas import tpu as pltpu
from jax.sharding import PartitionSpec as P

HD = 128
PAGE = 128
MESH = pl.DeviceIdType.MESH
masked_low = -1e30
f32 = jnp.float32
bf16 = jnp.bfloat16
inverse_square_root = 1.0 / math.sqrt(HD)


distance = (0, 1, 2, 1)
AROUND = sorted(
    ((z, y) for z in range(4) for y in range(4) if (z, y) != (0, 0)), key=lambda step: -distance[step[0]] - distance[step[1]]
)
COLUMN = (2, 1, 3)
GROUPS = (range(0, 5), range(5, 11), range(11, 15))
GROUP = [g for g, chips in enumerate(GROUPS) for _ in chips]


def step_by(chip, step, back=False):
    z, y = ((4 - step[0]) % 4, (4 - step[1]) % 4) if back else step
    return lax.rem(chip // 4 + z, 4) * 4 + lax.rem(lax.rem(chip, 4) + y, 4)


def project(hid, wq, wkv, part, part_kv):
    x = hid[...]
    for h in range(0, 16, 2):
        y = jnp.dot(x, wq[:, h * HD : (h + 2) * HD], preferred_element_type=f32)
        for c in range(2):
            for j in range(2):
                part[c, h + j] = y[32 * c : 32 * c + 32, HD * j : HD * j + HD]
    for b in range(0, 4, 2):
        y = jnp.dot(x, wkv[:, b * HD : (b + 2) * HD], preferred_element_type=f32)
        for c in range(2):
            for j in range(2):
                for rows in range(4):
                    at = 32 * c + 8 * rows
                    part_kv[c, rows * 4 + b + j] = y[at : at + 8, HD * j : HD * j + HD]


def each(low, high, step):
    def run(k, carry):
        step(k)
        return carry

    lax.fori_loop(low, high, run, 0)


def iota(shape, axis):
    return lax.broadcasted_iota(jnp.int32, shape, axis)


def page_table(cnt, slt, trm, ksv, vsv, sel, selt, nv, ks0, ks1, vs):
    zeros = jnp.zeros((1, 64), f32)
    count = jnp.concatenate([cnt[...].astype(f32), zeros], axis=1)
    trim = jnp.concatenate([trm[...].astype(f32), zeros], axis=1)
    i, j = iota((128, 128), 0), iota((128, 128), 1)
    count_col = jnp.sum(jnp.where(i == j, count, 0.0), axis=1, keepdims=True)
    end_col = jnp.sum(jnp.where(j <= i, count, 0.0), axis=1, keepdims=True)
    end = jnp.sum(jnp.where(i <= j, count_col, 0.0), axis=0, keepdims=True)
    start, start_col = end - count, end_col - count_col
    page = slt[...].astype(f32)

    def column(row):
        return jnp.sum(jnp.where(i == j, row, 0.0), axis=1, keepdims=True)

    page_col = column(page)
    mine = (start <= page_col) & (page_col < end)
    sel[...] = jnp.where(mine, 1.0, 0.0)
    selt[...] = jnp.where((start_col <= page) & (page < end_col), 1.0, 0.0)[:64].astype(bf16)
    left = PAGE * count - trim - PAGE * (page_col - start)
    valid = jnp.sum(jnp.where(mine, left, 0.0), axis=1, keepdims=True)
    nv[...] = jnp.broadcast_to(valid, (128, 128))
    ks0[...] = jnp.broadcast_to(column(ksv[0:1, :]) * inverse_square_root, (128, 128))
    ks1[...] = jnp.broadcast_to(column(ksv[1:2, :]) * inverse_square_root, (128, 128))
    for g in range(2):
        vs[g] = jnp.broadcast_to(column(vsv[g : g + 1, :]), (128, 128))


def select_query(h, qall, sel, qs):
    q = qall[pl.ds(2 * h, 2)].reshape(64, HD)
    at = pl.ds(pl.multiple_of(h * 128, 128), 128)
    qs[at, :] = jnp.dot(sel[:, 0:64].astype(bf16), q, preferred_element_type=f32)


def attend(slots, kc, vc, qs, nv, ks0, ks1, po, pm, ps):
    none = jnp.zeros((8, HD), f32)
    token = iota((16, PAGE), 1).astype(f32)
    scores, valids = [], []
    for slot in slots:
        q = qs[pl.ds(slot, 16, stride=128), :]
        left = jnp.concatenate([q[0:8], none], axis=0).astype(bf16)
        right = jnp.concatenate([none, q[8:16]], axis=0).astype(bf16)
        query = jnp.concatenate([left, right], axis=1)
        score = lax.dot_general(query, kc[slot], (((1,), (1,)), ((), ())), preferred_element_type=f32)
        scale0 = jnp.broadcast_to(ks0[pl.ds(slot, 1), :], (8, PAGE))
        scale1 = jnp.broadcast_to(ks1[pl.ds(slot, 1), :], (8, PAGE))
        score = score * jnp.concatenate([scale0, scale1], axis=0)
        valid = token < jnp.broadcast_to(nv[pl.ds(slot, 1), :], (16, PAGE))
        scores.append(jnp.where(valid, score, masked_low))
        valids.append(valid)
    tops = [jnp.max(score, axis=1, keepdims=True) for score in scores]
    probs = [
        jnp.where(valid, jnp.exp(score - top), 0.0).astype(bf16)
        for score, valid, top in zip(scores, valids, tops)
    ]
    totals = [jnp.sum(prob.astype(f32), axis=1, keepdims=True) for prob in probs]
    outs = [jnp.dot(prob, vc[slot], preferred_element_type=f32) for slot, prob in zip(slots, probs)]
    for slot, out, top, total in zip(slots, outs, tops, totals):
        at = pl.ds(pl.multiple_of(slot * 16, 16), 16)
        po[at, :] = jnp.concatenate([out[0:8, 0:HD], out[8:16, HD : 2 * HD]], axis=0)
        pm[at, :] = jnp.broadcast_to(top, (16, HD))
        ps[at, :] = jnp.broadcast_to(total, (16, HD))


def fold(h, sel, selt, vs, po, pm, ps, msg, stats):
    rows = pl.ds(h, 128, stride=16)
    mine = sel[...] > 0.5
    page_max = pm[rows, :]
    dev_max = jnp.max(jnp.where(mine, page_max, masked_low), axis=0, keepdims=True)
    slot_max = jnp.max(jnp.where(mine, dev_max, masked_low), axis=1, keepdims=True)
    weight = jnp.exp(page_max - slot_max)
    dev_sum = jnp.sum(jnp.where(mine, ps[rows, :] * weight, 0.0), axis=0, keepdims=True)
    stats[h] = jnp.concatenate([dev_max[:, 0:64], dev_sum[:, 0:64]], axis=1)
    weighted = (po[rows, :] * (weight * vs[h // 8])).astype(bf16)
    dev_out = jnp.dot(selt[...], weighted, preferred_element_type=f32).astype(bf16)
    for c in range(2):
        msg[2 * h + c] = dev_out[32 * c : 32 * c + 32]


def own_score(chip, qown, kvall):
    at = chip // 8 * 2
    new_key = jnp.concatenate([kvall[4 * r + at] for r in range(4)], axis=0)
    new_value = jnp.concatenate([kvall[4 * r + at + 1] for r in range(4)], axis=0)
    own = jnp.sum(qown[...].astype(f32) * new_key, axis=1, keepdims=True) * inverse_square_root
    return own, new_value


def finish(core, rmsg, rstats, own, new_value, flat, turned):
    stats = rstats[...].reshape(32, 128)
    cache_max = jnp.max(stats, axis=0, keepdims=True)
    factors = jnp.exp(stats - cache_max)
    sums = jnp.concatenate([stats[:, 64:128], stats[:, 0:64]], axis=1)
    flat[...] = jnp.zeros((128, 128), f32)
    flat[0:32] = factors
    flat[32:33] = cache_max
    flat[33:34] = jnp.sum(sums * factors, axis=0, keepdims=True)
    turned[...] = flat[...].T
    cols = turned[pl.ds(pl.multiple_of(core * 32, 32), 32), :]
    cache_out = jnp.zeros((32, HD), f32)
    for i in range(32):
        cache_out = cache_out + cols[:, i : i + 1] * rmsg[i].astype(f32)
    cache_max, cache_sum = cols[:, 32:33], cols[:, 33:34]
    top = jnp.maximum(cache_max, own)
    old_part = jnp.exp(cache_max - top)
    new_part = jnp.exp(own - top)
    denom = cache_sum * old_part + new_part
    return ((cache_out * old_part + new_part * new_value) / denom).astype(bf16)


def kernel(
    hidden_in, w_query, w_keyval, w_out, key_cache, value_cache, key_scale, value_scale, page_counts, slot_pages, trim,
    out_ref,
    hid, wq, wkv, wo, kc, vc, ksv, vsv, cnt, slt, trm,
    part, sib, rsb, part_kv, sib_kv, rsb_kv, qown, kvown, qall, kvall, qs, po, pm, ps, sel, selt, nv, ks0, ks1, vs,
    msg, rmsg, stats, rstats, flat, turned, ctx_own, ctx_all, xsend, xrecv,
    load_sem, sib_sem, send_sem, rs_recv, q_recv, kv_recv, o_recv, c_recv, x_recv, ready,
):
    me, col = lax.axis_index("seq"), lax.axis_index("head")
    chip, core = me // 2, lax.rem(me, 2)
    other = 1 - core
    sibling = 2 * chip + other

    def load(k, source, target):
        copy = pltpu.make_async_copy(source, target, load_sem.at[k])
        copy.start()
        return copy

    first = [load(0, hidden_in, hid), load(1, w_query, wq), load(2, w_keyval, wkv)]

    barrier = pltpu.get_barrier_semaphore()

    def greet(seq, head):
        pl.semaphore_signal(barrier, inc=1, device_id=(seq, head), device_id_type=MESH)

    row, line = chip // 4, lax.rem(chip, 4)

    def along_z(k):
        return 2 * (4 * lax.rem(row + k, 4) + line) + core

    for k in COLUMN:
        greet(2 * (4 * row + lax.rem(line + k, 4)) + core, col)
        greet(along_z(k), col)
        for c in range(2):
            greet(2 * chip + c, lax.rem(col + k, 4))
    greet(sibling, col)

    small = [
        load(3, page_counts, cnt), load(4, slot_pages, slt), load(5, trim, trm),
        load(6, key_scale, ksv), load(7, value_scale, vsv),
    ]
    for copy in first:
        copy.wait()
    keys, values, outs = load(8, key_cache, kc), load(9, value_cache, vc), load(10, w_out, wo.at[core])
    project(hid, wq, wkv, part, part_kv)

    def send(source, target, send_sem, recv_sem, seq, head=col):
        return pltpu.make_async_remote_copy(
            source, target, send_sem, recv_sem, device_id=(seq, head), device_id_type=MESH
        )

    pl.semaphore_wait(barrier, 13)
    for k in COLUMN:
        pl.semaphore_signal(ready, inc=1, device_id=(along_z(k), col), device_id_type=MESH)
    swap = send(part.at[other], sib, sib_sem.at[0], sib_sem.at[1], sibling)
    swap_kv = send(part_kv.at[other], sib_kv, sib_sem.at[2], sib_sem.at[3], sibling)
    swap.start()
    swap_kv.start()
    for copy in small:
        copy.wait()
    page_table(cnt, slt, trm, ksv, vsv, sel, selt, nv, ks0, ks1, vs)
    swap.wait_recv()
    sib[...] += part[core]
    pl.semaphore_wait(ready, 3)

    def landed(ref, semaphore):
        send(ref, ref, semaphore, semaphore, sibling).wait_recv()

    def left(ref, semaphore):
        send(ref, ref, semaphore, semaphore, sibling).wait_send()

    for i, step in enumerate(AROUND):
        peer = step_by(chip, step)
        send(sib.at[peer], rsb.at[i], send_sem.at[0], rs_recv.at[GROUP[i]], 2 * peer + core).start()
    swap_kv.wait_recv()
    sib_kv[...] += part_kv[core]
    total = sib[chip]
    for g in (2, 1, 0):
        landed(rsb.at[pl.ds(GROUPS[g][0], len(GROUPS[g]))], rs_recv.at[g])
        for i in GROUPS[g]:
            total = total + rsb[i]
    qown[...] = total.astype(bf16)

    for i, step in enumerate(AROUND):
        for c in range(2):
            peer = 2 * step_by(chip, step) + (other if c else core)
            send(qown, qall.at[me], send_sem.at[1], q_recv.at[GROUP[i]], peer).start()
    send(qown, qall.at[me], send_sem.at[1], q_recv.at[2], sibling).start()
    for i, step in enumerate(AROUND):
        peer = step_by(chip, step)
        send(sib_kv.at[peer], rsb_kv.at[i], send_sem.at[2], kv_recv.at[0], 2 * peer + core).start()
    qall[me] = qown[...]
    outs.wait()
    share = send(wo.at[core], wo.at[core], sib_sem.at[4], sib_sem.at[5], sibling)
    share.start()

    for g in (2, 1, 0):
        landed(qall.at[pl.ds(0, 2 * len(GROUPS[g]) + (g == 2))], q_recv.at[g])
        if g == 2:
            select_query(chip, qall, sel, qs)
        for i in GROUPS[g]:
            select_query(step_by(chip, AROUND[i], back=True), qall, sel, qs)
    landed(rsb_kv, kv_recv.at[0])
    total = sib_kv[chip]
    for i in range(15):
        total = total + rsb_kv[i]
    kvown[...] = total.astype(bf16).astype(f32)
    for i, step in enumerate(AROUND):
        peer = 2 * step_by(chip, step) + core
        send(kvown, kvall.at[chip], send_sem.at[3], kv_recv.at[1], peer).start()
    kvall[chip] = kvown[...]
    keys.wait()
    values.wait()

    def slots(k):
        attend([k * 32 + u for u in range(32)], kc, vc, qs, nv, ks0, ks1, po, pm, ps)

    each(0, 4, slots)

    for i in range(0, 15, 4):
        group = range(i, min(i + 4, 15))
        heads = {k: step_by(chip, AROUND[k]) for k in group}
        for k in group:
            fold(heads[k], sel, selt, vs, po, pm, ps, msg, stats)
        for k in group:
            for c in range(2):
                at = 2 * k + c
                peer = 2 * heads[k] + (other if c else core)
                send(msg.at[peer], rmsg.at[at], send_sem.at[4], o_recv.at[0], peer).start()
                send(stats.at[heads[k]], rstats.at[at], send_sem.at[5], o_recv.at[1], peer).start()
    fold(chip, sel, selt, vs, po, pm, ps, msg, stats)
    send(msg.at[sibling], rmsg.at[30], send_sem.at[4], o_recv.at[0], sibling).start()
    send(stats.at[chip], rstats.at[30], send_sem.at[5], o_recv.at[1], sibling).start()
    rmsg[31] = msg[me]
    rstats[31] = stats[chip]
    landed(kvall.at[pl.ds(0, 15)], kv_recv.at[1])
    own, new_value = own_score(chip, qown, kvall)
    landed(rstats.at[pl.ds(0, 31)], o_recv.at[1])
    landed(rmsg.at[pl.ds(0, 31)], o_recv.at[0])
    ctx_own[...] = finish(core, rmsg, rstats, own, new_value, flat, turned)

    for i, step in enumerate(AROUND):
        peer = 2 * step_by(chip, step) + core
        send(ctx_own, ctx_all.at[chip], send_sem.at[6], c_recv.at[GROUP[i]], peer).start()
    share.wait_send()
    landed(wo.at[other], sib_sem.at[5])

    def project_out(h, context, result):
        rows = pl.ds(pl.multiple_of(h * HD, HD), HD)
        return [y + jnp.dot(context, wo[c, rows, :], preferred_element_type=f32) for c, y in enumerate(result)]

    result = project_out(chip, ctx_own[...], [jnp.zeros((32, 256), f32)] * 2)
    for g in (2, 1, 0):
        landed(ctx_all.at[pl.ds(0, len(GROUPS[g]))], c_recv.at[g])
        for i in GROUPS[g]:
            source = step_by(chip, AROUND[i], back=True)
            result = project_out(source, ctx_all[source], result)
    for c in range(2):
        xsend[c] = result[c].astype(bf16)

    mine = 4 * core + col
    for k in COLUMN:
        for half in (core, other):
            there = lax.rem(col + k, 4)
            send(xsend.at[half], xrecv.at[mine], send_sem.at[7], x_recv.at[0], 2 * chip + half, there).start()
    send(xsend.at[other], xrecv.at[mine], send_sem.at[7], x_recv.at[0], sibling).start()
    xrecv[mine] = xsend[core]
    landed(xrecv.at[pl.ds(0, 7)], x_recv.at[0])
    for c in range(2):
        result = xrecv[4 * c].astype(f32)
        for k in range(1, 4):
            result = result + xrecv[4 * c + k].astype(f32)
        out_ref[32 * c : 32 * c + 32] = result.astype(bf16)

    swap.wait_send()
    swap_kv.wait_send()
    left(rsb, send_sem.at[0])
    left(qall.at[pl.ds(0, 31)], send_sem.at[1])
    left(rsb_kv, send_sem.at[2])
    left(kvall.at[pl.ds(0, 15)], send_sem.at[3])
    left(rmsg.at[pl.ds(0, 31)], send_sem.at[4])
    left(rstats.at[pl.ds(0, 31)], send_sem.at[5])
    left(ctx_all.at[pl.ds(0, 15)], send_sem.at[6])
    left(xrecv.at[pl.ds(0, 7)], send_sem.at[7])


def body(
    hidden_in, w_query, w_keyval, w_out, key_cache, value_cache, key_scale, value_scale, page_counts, slot_pages, trim
):
    vmem = pltpu.VMEM
    dma = pltpu.SemaphoreType.DMA
    return pl.pallas_call(
        kernel,
        out_shape=jax.ShapeDtypeStruct((64, 256), bf16),
        in_specs=[pl.BlockSpec(memory_space=pltpu.HBM)] * 11,
        out_specs=pl.BlockSpec(memory_space=pltpu.VMEM),
        scratch_shapes=[
            vmem((64, 256), bf16), vmem((256, 2048), bf16), vmem((256, 512), bf16), vmem((2, 2048, 256), bf16),
            vmem((128, PAGE, 256), bf16), vmem((128, PAGE, 256), bf16), vmem((2, 128), f32), vmem((2, 128), f32),
            vmem((1, 64), jnp.int32), vmem((1, 128), jnp.int32), vmem((1, 64), jnp.int32),
            vmem((2, 16, 32, HD), f32), vmem((16, 32, HD), f32), vmem((15, 32, HD), f32),
            vmem((2, 16, 8, HD), f32), vmem((16, 8, HD), f32), vmem((15, 8, HD), f32),
            vmem((32, HD), bf16), vmem((8, HD), f32), vmem((32, 32, HD), bf16), vmem((16, 8, HD), f32),
            vmem((2048, HD), f32), vmem((2048, HD), f32), vmem((2048, HD), f32), vmem((2048, HD), f32),
            vmem((128, 128), f32), vmem((64, 128), bf16), vmem((128, 128), f32),
            vmem((128, 128), f32), vmem((128, 128), f32), vmem((2, 128, 128), f32),
            vmem((32, 32, HD), bf16), vmem((32, 32, HD), bf16), vmem((16, 1, 128), f32), vmem((32, 1, 128), f32),
            vmem((128, 128), f32), vmem((128, 128), f32),
            vmem((32, HD), bf16), vmem((16, 32, HD), bf16), vmem((2, 32, 256), bf16), vmem((8, 32, 256), bf16),
            dma((11,)), dma((6,)), dma((8,)), dma((3,)), dma((3,)), dma((2,)), dma((2,)), dma((3,)), dma((1,)),
            pltpu.SemaphoreType.REGULAR,
        ],
        compiler_params=pltpu.CompilerParams(collective_id=0, has_side_effects=True, vmem_limit_bytes=63 << 20),
        cost_estimate=pl.CostEstimate(flops=300_000_000, bytes_accessed=20_000_000, transcendentals=300_000),
    )(
        hidden_in, w_query, w_keyval, w_out, key_cache, value_cache, key_scale.T, value_scale.T,
        page_counts.reshape(1, 64), slot_pages.reshape(1, 128), trim.reshape(1, 64),
    )


def solution(mesh):
    return jax.shard_map(
        body,
        mesh=mesh,
        in_specs=(
            P(None, "seq"),
            P("seq", "head"),
            P("seq", "head"),
            P("head", "seq"),
            P("seq", None, "head"),
            P("seq", None, "head"),
            P("seq", "head"),
            P("seq", "head"),
            P(),
            P("seq"),
            P(),
        ),
        out_specs=P(None, "seq"),
        check_vma=False,
    )
```

```python
import functools
import math

import jax
import jax.numpy as jnp
from jax import lax
from jax.experimental import pallas as pl
from jax.experimental.pallas import tpu as pltpu
from jax.sharding import PartitionSpec as P

HD = 128
PAGE = 128
MESH = pl.DeviceIdType.MESH
masked_low = -1e30
f32 = jnp.float32
bf16 = jnp.bfloat16
inverse_square_root = 1.0 / math.sqrt(HD)


distance = (0, 1, 2, 1)
AROUND = sorted(
    ((z, y) for z in range(4) for y in range(4) if (z, y) != (0, 0)), key=lambda step: -distance[step[0]] - distance[step[1]]
)
COLUMN = (2, 1, 3)
GROUPS = (range(0, 5), range(5, 11), range(11, 15))
GROUP = [g for g, chips in enumerate(GROUPS) for _ in chips]


def step_by(chip, step, back=False):
    z, y = ((4 - step[0]) % 4, (4 - step[1]) % 4) if back else step
    return lax.rem(chip // 4 + z, 4) * 4 + lax.rem(lax.rem(chip, 4) + y, 4)


def project(hid, wq, wkv, part, part_kv):
    x = hid[...]
    for h in range(0, 16, 2):
        y = jnp.dot(x, wq[:, h * HD : (h + 2) * HD], preferred_element_type=f32)
        for c in range(2):
            for j in range(2):
                part[c, h + j] = y[32 * c : 32 * c + 32, HD * j : HD * j + HD]
    for b in range(0, 4, 2):
        y = jnp.dot(x, wkv[:, b * HD : (b + 2) * HD], preferred_element_type=f32)
        for c in range(2):
            for j in range(2):
                for rows in range(4):
                    at = 32 * c + 8 * rows
                    part_kv[c, rows * 4 + b + j] = y[at : at + 8, HD * j : HD * j + HD]


def iota(shape, axis):
    return lax.broadcasted_iota(jnp.int32, shape, axis)


def page_table(cnt, slt, trm, ksv, vsv, sel, selt, nv, ks0, ks1, vs):
    zeros = jnp.zeros((1, 64), f32)
    count = jnp.concatenate([cnt[...].astype(f32), zeros], axis=1)
    trim = jnp.concatenate([trm[...].astype(f32), zeros], axis=1)
    i, j = iota((128, 128), 0), iota((128, 128), 1)
    count_col = jnp.sum(jnp.where(i == j, count, 0.0), axis=1, keepdims=True)
    end_col = jnp.sum(jnp.where(j <= i, count, 0.0), axis=1, keepdims=True)
    end = jnp.sum(jnp.where(i <= j, count_col, 0.0), axis=0, keepdims=True)
    start, start_col = end - count, end_col - count_col
    page = slt[...].astype(f32)

    def column(row):
        return jnp.sum(jnp.where(i == j, row, 0.0), axis=1, keepdims=True)

    page_col = column(page)
    mine = (start <= page_col) & (page_col < end)
    sel[...] = jnp.where(mine, 1.0, 0.0)
    selt[...] = jnp.where((start_col <= page) & (page < end_col), 1.0, 0.0)[:64].astype(bf16)
    left = PAGE * count - trim - PAGE * (page_col - start)
    valid = jnp.sum(jnp.where(mine, left, 0.0), axis=1, keepdims=True)
    nv[...] = jnp.broadcast_to(valid, (128, 128))
    ks0[...] = jnp.broadcast_to(column(ksv[0:1, :]) * inverse_square_root, (128, 128))
    ks1[...] = jnp.broadcast_to(column(ksv[1:2, :]) * inverse_square_root, (128, 128))
    for g in range(2):
        vs[g] = jnp.broadcast_to(column(vsv[g : g + 1, :]), (128, 128))


def select_query(h, qall, sel, qs):
    q = qall[pl.ds(2 * h, 2)].reshape(64, HD)
    at = pl.ds(pl.multiple_of(h * 128, 128), 128)
    qs[at, :] = jnp.dot(sel[:, 0:64].astype(bf16), q, preferred_element_type=f32)


def turn_keys(kc):
    def some(k, carry):
        for u in range(16):
            slot = k * 16 + u
            kc[slot] = jnp.concatenate([kc[slot, :, 0:HD].T, kc[slot, :, HD : 2 * HD].T], axis=1)
        return carry

    lax.fori_loop(0, 8, some, 0)


def attend(slots, kc, vc, qs, nv, ks0, ks1, po, pm, ps):
    token = iota((16, PAGE), 1).astype(f32)
    scores, valids = [], []
    for slot in slots:
        query = qs[pl.ds(slot, 16, stride=128), :].astype(bf16)
        score = jnp.dot(query, kc[slot], preferred_element_type=f32)
        score = jnp.concatenate([score[0:8, 0:PAGE], score[8:16, PAGE : 2 * PAGE]], axis=0)
        scale0 = jnp.broadcast_to(ks0[pl.ds(slot, 1), :], (8, PAGE))
        scale1 = jnp.broadcast_to(ks1[pl.ds(slot, 1), :], (8, PAGE))
        score = score * jnp.concatenate([scale0, scale1], axis=0)
        valid = token < jnp.broadcast_to(nv[pl.ds(slot, 1), :], (16, PAGE))
        scores.append(jnp.where(valid, score, masked_low))
        valids.append(valid)
    tops = [jnp.max(score, axis=1, keepdims=True) for score in scores]
    probs = [
        jnp.where(valid, jnp.exp(score - top), 0.0).astype(bf16)
        for score, valid, top in zip(scores, valids, tops)
    ]
    totals = [jnp.sum(prob.astype(f32), axis=1, keepdims=True) for prob in probs]
    outs = [jnp.dot(prob, vc[slot], preferred_element_type=f32) for slot, prob in zip(slots, probs)]
    for slot, out, top, total in zip(slots, outs, tops, totals):
        at = slice(slot * 16, slot * 16 + 16)
        po[at, :] = jnp.concatenate([out[0:8, 0:HD], out[8:16, HD : 2 * HD]], axis=0)
        pm[at, :] = jnp.broadcast_to(top, (16, HD))
        ps[at, :] = jnp.broadcast_to(total, (16, HD))


def fold(h, sel, selt, vs, po, pm, ps, msg, stats):
    rows = pl.ds(h, 128, stride=16)
    mine = sel[...] > 0.5
    page_max = pm[rows, :]
    dev_max = jnp.max(jnp.where(mine, page_max, masked_low), axis=0, keepdims=True)
    slot_max = jnp.max(jnp.where(mine, dev_max, masked_low), axis=1, keepdims=True)
    weight = jnp.exp(page_max - slot_max)
    dev_sum = jnp.sum(jnp.where(mine, ps[rows, :] * weight, 0.0), axis=0, keepdims=True)
    stats[h] = jnp.concatenate([dev_max[:, 0:64], dev_sum[:, 0:64]], axis=1)
    weighted = (po[rows, :] * (weight * vs[h // 8])).astype(bf16)
    dev_out = jnp.dot(selt[...], weighted, preferred_element_type=f32).astype(bf16)
    for c in range(2):
        msg[2 * h + c] = dev_out[32 * c : 32 * c + 32]


def own_score(chip, qown, kvall):
    at = chip // 8 * 2
    new_key = jnp.concatenate([kvall[4 * r + at] for r in range(4)], axis=0)
    new_value = jnp.concatenate([kvall[4 * r + at + 1] for r in range(4)], axis=0)
    own = jnp.sum(qown[...].astype(f32) * new_key, axis=1, keepdims=True) * inverse_square_root
    return own, new_value


def finish(core, rmsg, rstats, own, new_value, flat, turned):
    stats = rstats[...].reshape(32, 128)
    cache_max = jnp.max(stats, axis=0, keepdims=True)
    factors = jnp.exp(stats - cache_max)
    sums = jnp.concatenate([stats[:, 64:128], stats[:, 0:64]], axis=1)
    flat[...] = jnp.zeros((128, 128), f32)
    flat[0:32] = factors
    flat[32:33] = cache_max
    flat[33:34] = jnp.sum(sums * factors, axis=0, keepdims=True)
    turned[...] = flat[...].T
    cols = turned[pl.ds(pl.multiple_of(core * 32, 32), 32), :]
    cache_out = jnp.zeros((32, HD), f32)
    for i in range(32):
        cache_out = cache_out + cols[:, i : i + 1] * rmsg[i].astype(f32)
    cache_max, cache_sum = cols[:, 32:33], cols[:, 33:34]
    top = jnp.maximum(cache_max, own)
    old_part = jnp.exp(cache_max - top)
    new_part = jnp.exp(own - top)
    denom = cache_sum * old_part + new_part
    return ((cache_out * old_part + new_part * new_value) / denom).astype(bf16)


def kernel(
    hidden_in, w_query, w_keyval, w_out, key_cache, value_cache, key_scale, value_scale, page_counts, slot_pages, trim,
    out_ref,
    hid, wq, wkv, wo, kc, vc, ksv, vsv, cnt, slt, trm,
    part, sib, rsb, part_kv, sib_kv, rsb_kv, qown, kvown, qall, kvall, qs, po, pm, ps, sel, selt, nv, ks0, ks1, vs,
    msg, rmsg, stats, rstats, flat, turned, ctx_own, ctx_all, xsend, xrecv,
    load_sem, sib_sem, send_sem, rs_recv, q_recv, kv_recv, o_recv, c_recv, x_recv, ready,
):
    me, col = lax.axis_index("seq"), lax.axis_index("head")
    chip, core = me // 2, lax.rem(me, 2)
    other = 1 - core
    sibling = 2 * chip + other

    def load(k, source, target):
        copy = pltpu.make_async_copy(source, target, load_sem.at[k])
        copy.start()
        return copy

    first = [load(0, hidden_in, hid), load(1, w_query, wq), load(2, w_keyval, wkv)]

    barrier = pltpu.get_barrier_semaphore()

    def greet(seq, head):
        pl.semaphore_signal(barrier, inc=1, device_id=(seq, head), device_id_type=MESH)

    row, line = chip // 4, lax.rem(chip, 4)

    def along_z(k):
        return 2 * (4 * lax.rem(row + k, 4) + line) + core

    for k in COLUMN:
        greet(2 * (4 * row + lax.rem(line + k, 4)) + core, col)
        greet(along_z(k), col)
        for c in range(2):
            greet(2 * chip + c, lax.rem(col + k, 4))
    greet(sibling, col)

    small = [
        load(3, page_counts, cnt), load(4, slot_pages, slt), load(5, trim, trm),
        load(6, key_scale, ksv), load(7, value_scale, vsv),
    ]
    for copy in first:
        copy.wait()
    keys, values, outs = load(8, key_cache, kc), load(9, value_cache, vc), load(10, w_out, wo.at[core])
    project(hid, wq, wkv, part, part_kv)

    def send(source, target, send_sem, recv_sem, seq, head=col):
        return pltpu.make_async_remote_copy(
            source, target, send_sem, recv_sem, device_id=(seq, head), device_id_type=MESH
        )

    pl.semaphore_wait(barrier, 13)
    for k in COLUMN:
        pl.semaphore_signal(ready, inc=1, device_id=(along_z(k), col), device_id_type=MESH)
    swap = send(part.at[other], sib, sib_sem.at[0], sib_sem.at[1], sibling)
    swap_kv = send(part_kv.at[other], sib_kv, sib_sem.at[2], sib_sem.at[3], sibling)
    swap.start()
    swap_kv.start()
    for copy in small:
        copy.wait()
    page_table(cnt, slt, trm, ksv, vsv, sel, selt, nv, ks0, ks1, vs)
    swap.wait_recv()
    sib[...] += part[core]

    def landed(ref, semaphore):
        send(ref, ref, semaphore, semaphore, sibling).wait_recv()

    def left(ref, semaphore):
        send(ref, ref, semaphore, semaphore, sibling).wait_send()

    def reduce_to(i):
        peer = step_by(chip, AROUND[i])
        send(sib.at[peer], rsb.at[i], send_sem.at[0], rs_recv.at[GROUP[i]], 2 * peer + core).start()

    pl.semaphore_wait(ready, 3)
    for i in range(15):
        reduce_to(i)
    swap_kv.wait_recv()
    sib_kv[...] += part_kv[core]
    keys.wait()
    turn_keys(kc)
    total = sib[chip]
    for g in (2, 1, 0):
        landed(rsb.at[pl.ds(GROUPS[g][0], len(GROUPS[g]))], rs_recv.at[g])
        for i in GROUPS[g]:
            total = total + rsb[i]
    qown[...] = total.astype(bf16)

    for i, step in enumerate(AROUND):
        for c in range(2):
            peer = 2 * step_by(chip, step) + (other if c else core)
            send(qown, qall.at[me], send_sem.at[1], q_recv.at[GROUP[i]], peer).start()
    send(qown, qall.at[me], send_sem.at[1], q_recv.at[2], sibling).start()
    for i, step in enumerate(AROUND):
        peer = step_by(chip, step)
        send(sib_kv.at[peer], rsb_kv.at[i], send_sem.at[2], kv_recv.at[0], 2 * peer + core).start()
    qall[me] = qown[...]
    outs.wait()
    share = send(wo.at[core], wo.at[core], sib_sem.at[4], sib_sem.at[5], sibling)
    share.start()

    for g in (2, 1, 0):
        landed(qall.at[pl.ds(0, 2 * len(GROUPS[g]) + (g == 2))], q_recv.at[g])
        if g == 2:
            select_query(chip, qall, sel, qs)
        for i in GROUPS[g]:
            select_query(step_by(chip, AROUND[i], back=True), qall, sel, qs)
    values.wait()

    attend(range(0, 64), kc, vc, qs, nv, ks0, ks1, po, pm, ps)
    landed(rsb_kv, kv_recv.at[0])
    total = sib_kv[chip]
    for i in range(15):
        total = total + rsb_kv[i]
    kvown[...] = total.astype(bf16).astype(f32)
    for i, step in enumerate(AROUND):
        peer = 2 * step_by(chip, step) + core
        send(kvown, kvall.at[chip], send_sem.at[3], kv_recv.at[1], peer).start()
    kvall[chip] = kvown[...]
    attend(range(64, 128), kc, vc, qs, nv, ks0, ks1, po, pm, ps)

    for i in range(0, 15, 4):
        group = range(i, min(i + 4, 15))
        heads = {k: step_by(chip, AROUND[k]) for k in group}
        for k in group:
            fold(heads[k], sel, selt, vs, po, pm, ps, msg, stats)
        for k in group:
            for c in range(2):
                at = 2 * k + c
                peer = 2 * heads[k] + (other if c else core)
                send(msg.at[peer], rmsg.at[at], send_sem.at[4], o_recv.at[0], peer).start()
                send(stats.at[heads[k]], rstats.at[at], send_sem.at[5], o_recv.at[1], peer).start()
    fold(chip, sel, selt, vs, po, pm, ps, msg, stats)
    send(msg.at[sibling], rmsg.at[30], send_sem.at[4], o_recv.at[0], sibling).start()
    send(stats.at[chip], rstats.at[30], send_sem.at[5], o_recv.at[1], sibling).start()
    rmsg[31] = msg[me]
    rstats[31] = stats[chip]
    landed(kvall.at[pl.ds(0, 15)], kv_recv.at[1])
    own, new_value = own_score(chip, qown, kvall)
    landed(rstats.at[pl.ds(0, 31)], o_recv.at[1])
    landed(rmsg.at[pl.ds(0, 31)], o_recv.at[0])
    ctx_own[...] = finish(core, rmsg, rstats, own, new_value, flat, turned)

    for i, step in enumerate(AROUND):
        peer = 2 * step_by(chip, step) + core
        send(ctx_own, ctx_all.at[chip], send_sem.at[6], c_recv.at[GROUP[i]], peer).start()
    share.wait_send()
    landed(wo.at[other], sib_sem.at[5])

    def project_out(h, context, result):
        rows = pl.ds(pl.multiple_of(h * HD, HD), HD)
        return [y + jnp.dot(context, wo[c, rows, :], preferred_element_type=f32) for c, y in enumerate(result)]

    result = project_out(chip, ctx_own[...], [jnp.zeros((32, 256), f32)] * 2)
    for g in (2, 1, 0):
        landed(ctx_all.at[pl.ds(0, len(GROUPS[g]))], c_recv.at[g])
        for i in GROUPS[g]:
            source = step_by(chip, AROUND[i], back=True)
            result = project_out(source, ctx_all[source], result)
    for c in range(2):
        xsend[c] = result[c].astype(bf16)

    mine = 4 * core + col
    for k in COLUMN:
        for half in (core, other):
            there = lax.rem(col + k, 4)
            send(xsend.at[half], xrecv.at[mine], send_sem.at[7], x_recv.at[0], 2 * chip + half, there).start()
    send(xsend.at[other], xrecv.at[mine], send_sem.at[7], x_recv.at[0], sibling).start()
    xrecv[mine] = xsend[core]
    landed(xrecv.at[pl.ds(0, 7)], x_recv.at[0])
    for c in range(2):
        result = xrecv[4 * c].astype(f32)
        for k in range(1, 4):
            result = result + xrecv[4 * c + k].astype(f32)
        out_ref[32 * c : 32 * c + 32] = result.astype(bf16)

    swap.wait_send()
    swap_kv.wait_send()
    left(rsb, send_sem.at[0])
    left(qall.at[pl.ds(0, 31)], send_sem.at[1])
    left(rsb_kv, send_sem.at[2])
    left(kvall.at[pl.ds(0, 15)], send_sem.at[3])
    left(rmsg.at[pl.ds(0, 31)], send_sem.at[4])
    left(rstats.at[pl.ds(0, 31)], send_sem.at[5])
    left(ctx_all.at[pl.ds(0, 15)], send_sem.at[6])
    left(xrecv.at[pl.ds(0, 7)], send_sem.at[7])


def body(
    hidden_in, w_query, w_keyval, w_out, key_cache, value_cache, key_scale, value_scale, page_counts, slot_pages, trim
):
    vmem = pltpu.VMEM
    dma = pltpu.SemaphoreType.DMA
    return pl.pallas_call(
        kernel,
        out_shape=jax.ShapeDtypeStruct((64, 256), bf16),
        in_specs=[pl.BlockSpec(memory_space=pltpu.HBM)] * 11,
        out_specs=pl.BlockSpec(memory_space=pltpu.VMEM),
        scratch_shapes=[
            vmem((64, 256), bf16), vmem((256, 2048), bf16), vmem((256, 512), bf16), vmem((2, 2048, 256), bf16),
            vmem((128, PAGE, 256), bf16), vmem((128, PAGE, 256), bf16), vmem((2, 128), f32), vmem((2, 128), f32),
            vmem((1, 64), jnp.int32), vmem((1, 128), jnp.int32), vmem((1, 64), jnp.int32),
            vmem((2, 16, 32, HD), f32), vmem((16, 32, HD), f32), vmem((15, 32, HD), f32),
            vmem((2, 16, 8, HD), f32), vmem((16, 8, HD), f32), vmem((15, 8, HD), f32),
            vmem((32, HD), bf16), vmem((8, HD), f32), vmem((32, 32, HD), bf16), vmem((16, 8, HD), f32),
            vmem((2048, HD), f32), vmem((2048, HD), f32), vmem((2048, HD), f32), vmem((2048, HD), f32),
            vmem((128, 128), f32), vmem((64, 128), bf16), vmem((128, 128), f32),
            vmem((128, 128), f32), vmem((128, 128), f32), vmem((2, 128, 128), f32),
            vmem((32, 32, HD), bf16), vmem((32, 32, HD), bf16), vmem((16, 1, 128), f32), vmem((32, 1, 128), f32),
            vmem((128, 128), f32), vmem((128, 128), f32),
            vmem((32, HD), bf16), vmem((16, 32, HD), bf16), vmem((2, 32, 256), bf16), vmem((8, 32, 256), bf16),
            dma((11,)), dma((6,)), dma((8,)), dma((3,)), dma((3,)), dma((2,)), dma((2,)), dma((3,)), dma((1,)),
            pltpu.SemaphoreType.REGULAR,
        ],
        compiler_params=pltpu.CompilerParams(collective_id=0, has_side_effects=True, vmem_limit_bytes=63 << 20),
        cost_estimate=pl.CostEstimate(flops=300_000_000, bytes_accessed=20_000_000, transcendentals=300_000),
    )(
        hidden_in, w_query, w_keyval, w_out, key_cache, value_cache, key_scale.T, value_scale.T,
        page_counts.reshape(1, 64), slot_pages.reshape(1, 128), trim.reshape(1, 64),
    )


def solution(mesh):
    return jax.shard_map(
        body,
        mesh=mesh,
        in_specs=(
            P(None, "seq"),
            P("seq", "head"),
            P("seq", "head"),
            P("head", "seq"),
            P("seq", None, "head"),
            P("seq", None, "head"),
            P("seq", "head"),
            P("seq", "head"),
            P(),
            P("seq"),
            P(),
        ),
        out_specs=P(None, "seq"),
        check_vma=False,
    )
```

```python
import functools
import math

import jax
import jax.numpy as jnp
from jax import lax
from jax.experimental import pallas as pl
from jax.experimental.pallas import tpu as pltpu
from jax.sharding import PartitionSpec as P

HD = 128
PAGE = 128
MESH = pl.DeviceIdType.MESH
masked_low = -1e30
f32 = jnp.float32
bf16 = jnp.bfloat16
inverse_square_root = 1.0 / math.sqrt(HD)


distance = (0, 1, 2, 1)
AROUND = sorted(
    ((z, y) for z in range(4) for y in range(4) if (z, y) != (0, 0)), key=lambda step: -distance[step[0]] - distance[step[1]]
)
COLUMN = (2, 1, 3)
GROUPS = (range(0, 5), range(5, 11), range(11, 15))
GROUP = [g for g, chips in enumerate(GROUPS) for _ in chips]


def step_by(chip, step, back=False):
    z, y = ((4 - step[0]) % 4, (4 - step[1]) % 4) if back else step
    return lax.rem(chip // 4 + z, 4) * 4 + lax.rem(lax.rem(chip, 4) + y, 4)


def project(hid, wq, wkv, part, part_kv):
    x = hid[...]
    for h in range(0, 16, 2):
        y = jnp.dot(x, wq[:, h * HD : (h + 2) * HD], preferred_element_type=f32)
        for c in range(2):
            for j in range(2):
                part[c, h + j] = y[32 * c : 32 * c + 32, HD * j : HD * j + HD]
    for b in range(0, 4, 2):
        y = jnp.dot(x, wkv[:, b * HD : (b + 2) * HD], preferred_element_type=f32)
        for c in range(2):
            for j in range(2):
                for rows in range(4):
                    at = 32 * c + 8 * rows
                    part_kv[c, rows * 4 + b + j] = y[at : at + 8, HD * j : HD * j + HD]


def iota(shape, axis):
    return lax.broadcasted_iota(jnp.int32, shape, axis)


def page_table(cnt, slt, trm, ksv, vsv, sel, selt, nv, ks0, ks1, vs):
    zeros = jnp.zeros((1, 64), f32)
    count = jnp.concatenate([cnt[...].astype(f32), zeros], axis=1)
    trim = jnp.concatenate([trm[...].astype(f32), zeros], axis=1)
    i, j = iota((128, 128), 0), iota((128, 128), 1)
    count_col = jnp.sum(jnp.where(i == j, count, 0.0), axis=1, keepdims=True)
    end_col = jnp.sum(jnp.where(j <= i, count, 0.0), axis=1, keepdims=True)
    end = jnp.sum(jnp.where(i <= j, count_col, 0.0), axis=0, keepdims=True)
    start, start_col = end - count, end_col - count_col
    page = slt[...].astype(f32)

    def column(row):
        return jnp.sum(jnp.where(i == j, row, 0.0), axis=1, keepdims=True)

    page_col = column(page)
    mine = (start <= page_col) & (page_col < end)
    sel[...] = jnp.where(mine, 1.0, 0.0)
    selt[...] = jnp.where((start_col <= page) & (page < end_col), 1.0, 0.0)[:64].astype(bf16)
    left = PAGE * count - trim - PAGE * (page_col - start)
    valid = jnp.sum(jnp.where(mine, left, 0.0), axis=1, keepdims=True)
    nv[...] = jnp.broadcast_to(valid, (128, 128))
    ks0[...] = jnp.broadcast_to(column(ksv[0:1, :]) * inverse_square_root, (128, 128))
    ks1[...] = jnp.broadcast_to(column(ksv[1:2, :]) * inverse_square_root, (128, 128))
    for g in range(2):
        vs[g] = jnp.broadcast_to(column(vsv[g : g + 1, :]), (128, 128))


def select_query(h, qall, sel, qs):
    q = qall[pl.ds(2 * h, 2)].reshape(64, HD)
    at = pl.ds(pl.multiple_of(h * 128, 128), 128)
    qs[at, :] = jnp.dot(sel[:, 0:64].astype(bf16), q, preferred_element_type=f32)


def turn_keys(kc):
    def some(k, carry):
        for u in range(16):
            slot = k * 16 + u
            kc[slot] = jnp.concatenate([kc[slot, :, 0:HD].T, kc[slot, :, HD : 2 * HD].T], axis=1)
        return carry

    lax.fori_loop(0, 8, some, 0)


def attend(slots, kc, vc, qs, nv, ks0, ks1, po, pm, ps):
    token = iota((16, PAGE), 1).astype(f32)
    scores, valids = [], []
    for slot in slots:
        query = qs[pl.ds(slot, 16, stride=128), :].astype(bf16)
        score = jnp.dot(query, kc[slot], preferred_element_type=f32)
        score = jnp.concatenate([score[0:8, 0:PAGE], score[8:16, PAGE : 2 * PAGE]], axis=0)
        scale0 = jnp.broadcast_to(ks0[pl.ds(slot, 1), :], (8, PAGE))
        scale1 = jnp.broadcast_to(ks1[pl.ds(slot, 1), :], (8, PAGE))
        score = score * jnp.concatenate([scale0, scale1], axis=0)
        valid = token < jnp.broadcast_to(nv[pl.ds(slot, 1), :], (16, PAGE))
        scores.append(jnp.where(valid, score, masked_low))
        valids.append(valid)
    tops = [jnp.max(score, axis=1, keepdims=True) for score in scores]
    probs = [
        jnp.where(valid, jnp.exp(score - top), 0.0).astype(bf16)
        for score, valid, top in zip(scores, valids, tops)
    ]
    totals = [jnp.sum(prob.astype(f32), axis=1, keepdims=True) for prob in probs]
    outs = [jnp.dot(prob, vc[slot], preferred_element_type=f32) for slot, prob in zip(slots, probs)]
    for slot, out, top, total in zip(slots, outs, tops, totals):
        at = slice(slot * 16, slot * 16 + 16)
        po[at, :] = jnp.concatenate([out[0:8, 0:HD], out[8:16, HD : 2 * HD]], axis=0)
        pm[at, :] = jnp.broadcast_to(top, (16, HD))
        ps[at, :] = jnp.broadcast_to(total, (16, HD))


def fold(h, sel, selt, vs, po, pm, ps, msg, stats):
    rows = pl.ds(h, 128, stride=16)
    mine = sel[...] > 0.5
    page_max = pm[rows, :]
    dev_max = jnp.max(jnp.where(mine, page_max, masked_low), axis=0, keepdims=True)
    slot_max = jnp.max(jnp.where(mine, dev_max, masked_low), axis=1, keepdims=True)
    weight = jnp.exp(page_max - slot_max)
    dev_sum = jnp.sum(jnp.where(mine, ps[rows, :] * weight, 0.0), axis=0, keepdims=True)
    stats[h] = jnp.concatenate([dev_max[:, 0:64], dev_sum[:, 0:64]], axis=1)
    weighted = (po[rows, :] * (weight * vs[h // 8])).astype(bf16)
    dev_out = jnp.dot(selt[...], weighted, preferred_element_type=f32).astype(bf16)
    for c in range(2):
        msg[2 * h + c] = dev_out[32 * c : 32 * c + 32]


def own_score(chip, qown, kvall):
    at = chip // 8 * 2
    new_key = jnp.concatenate([kvall[4 * r + at] for r in range(4)], axis=0)
    new_value = jnp.concatenate([kvall[4 * r + at + 1] for r in range(4)], axis=0)
    own = jnp.sum(qown[...].astype(f32) * new_key, axis=1, keepdims=True) * inverse_square_root
    return own, new_value


def finish(core, rmsg, rstats, own, new_value, flat, turned):
    stats = rstats[...].reshape(32, 128)
    cache_max = jnp.max(stats, axis=0, keepdims=True)
    factors = jnp.exp(stats - cache_max)
    sums = jnp.concatenate([stats[:, 64:128], stats[:, 0:64]], axis=1)
    flat[...] = jnp.zeros((128, 128), f32)
    flat[0:32] = factors
    flat[32:33] = cache_max
    flat[33:34] = jnp.sum(sums * factors, axis=0, keepdims=True)
    turned[...] = flat[...].T
    cols = turned[pl.ds(pl.multiple_of(core * 32, 32), 32), :]
    cache_out = jnp.zeros((32, HD), f32)
    for i in range(32):
        cache_out = cache_out + cols[:, i : i + 1] * rmsg[i].astype(f32)
    cache_max, cache_sum = cols[:, 32:33], cols[:, 33:34]
    top = jnp.maximum(cache_max, own)
    old_part = jnp.exp(cache_max - top)
    new_part = jnp.exp(own - top)
    denom = cache_sum * old_part + new_part
    return ((cache_out * old_part + new_part * new_value) / denom).astype(bf16)


def kernel(
    hidden_in, w_query, w_keyval, w_out, key_cache, value_cache, key_scale, value_scale, page_counts, slot_pages, trim,
    out_ref,
    hid, wq, wkv, wo, kc, vc, ksv, vsv, cnt, slt, trm,
    part, sib, rsb, part_kv, sib_kv, rsb_kv, qown, kvown, qall, kvall, qs, po, pm, ps, sel, selt, nv, ks0, ks1, vs,
    msg, rmsg, stats, rstats, flat, turned, ctx_own, ctx_all, xsend, xrecv,
    load_sem, sib_sem, send_sem, rs_recv, q_recv, kv_recv, o_recv, c_recv, x_recv, ready,
):
    me, col = lax.axis_index("seq"), lax.axis_index("head")
    chip, core = me // 2, lax.rem(me, 2)
    other = 1 - core
    sibling = 2 * chip + other

    def load(k, source, target):
        copy = pltpu.make_async_copy(source, target, load_sem.at[k])
        copy.start()
        return copy

    first = [load(0, hidden_in, hid), load(1, w_query, wq), load(2, w_keyval, wkv)]

    barrier = pltpu.get_barrier_semaphore()

    def greet(seq, head):
        pl.semaphore_signal(barrier, inc=1, device_id=(seq, head), device_id_type=MESH)

    row, line = chip // 4, lax.rem(chip, 4)

    def along_z(k):
        return 2 * (4 * lax.rem(row + k, 4) + line) + core

    for k in COLUMN:
        greet(2 * (4 * row + lax.rem(line + k, 4)) + core, col)
        greet(along_z(k), col)
        for c in range(2):
            greet(2 * chip + c, lax.rem(col + k, 4))
    greet(sibling, col)

    small = [
        load(3, page_counts, cnt), load(4, slot_pages, slt), load(5, trim, trm),
        load(6, key_scale, ksv), load(7, value_scale, vsv),
    ]
    for copy in first:
        copy.wait()
    keys, values, outs = load(8, key_cache, kc), load(9, value_cache, vc), load(10, w_out, wo.at[core])
    project(hid, wq, wkv, part, part_kv)

    def send(source, target, send_sem, recv_sem, seq, head=col):
        return pltpu.make_async_remote_copy(
            source, target, send_sem, recv_sem, device_id=(seq, head), device_id_type=MESH
        )

    pl.semaphore_wait(barrier, 13)
    for k in COLUMN:
        pl.semaphore_signal(ready, inc=1, device_id=(along_z(k), col), device_id_type=MESH)
    swap = send(part.at[other], sib, sib_sem.at[0], sib_sem.at[1], sibling)
    swap_kv = send(part_kv.at[other], sib_kv, sib_sem.at[2], sib_sem.at[3], sibling)
    swap.start()
    swap_kv.start()
    for copy in small:
        copy.wait()
    page_table(cnt, slt, trm, ksv, vsv, sel, selt, nv, ks0, ks1, vs)
    swap.wait_recv()
    sib[...] += part[core]

    def landed(ref, semaphore):
        send(ref, ref, semaphore, semaphore, sibling).wait_recv()

    def left(ref, semaphore):
        send(ref, ref, semaphore, semaphore, sibling).wait_send()

    def reduce_to(i):
        peer = step_by(chip, AROUND[i])
        send(sib.at[peer], rsb.at[i], send_sem.at[0], rs_recv.at[GROUP[i]], 2 * peer + core).start()

    pl.semaphore_wait(ready, 3)
    for i in range(15):
        reduce_to(i)
    swap_kv.wait_recv()
    sib_kv[...] += part_kv[core]
    keys.wait()
    turn_keys(kc)
    total = sib[chip]
    for g in (2, 1, 0):
        landed(rsb.at[pl.ds(GROUPS[g][0], len(GROUPS[g]))], rs_recv.at[g])
        for i in GROUPS[g]:
            total = total + rsb[i]
    qown[...] = total.astype(bf16)

    for i, step in enumerate(AROUND):
        for c in range(2):
            peer = 2 * step_by(chip, step) + (other if c else core)
            send(qown, qall.at[me], send_sem.at[1], q_recv.at[GROUP[i]], peer).start()
    send(qown, qall.at[me], send_sem.at[1], q_recv.at[2], sibling).start()
    for i, step in enumerate(AROUND):
        peer = step_by(chip, step)
        send(sib_kv.at[peer], rsb_kv.at[i], send_sem.at[2], kv_recv.at[0], 2 * peer + core).start()
    qall[me] = qown[...]
    outs.wait()
    share = send(wo.at[core], wo.at[core], sib_sem.at[4], sib_sem.at[5], sibling)
    share.start()

    for g in (2, 1, 0):
        landed(qall.at[pl.ds(0, 2 * len(GROUPS[g]) + (g == 2))], q_recv.at[g])
        if g == 2:
            select_query(chip, qall, sel, qs)
        for i in GROUPS[g]:
            select_query(step_by(chip, AROUND[i], back=True), qall, sel, qs)
    values.wait()

    attend(range(0, 64), kc, vc, qs, nv, ks0, ks1, po, pm, ps)
    landed(rsb_kv, kv_recv.at[0])
    total = sib_kv[chip]
    for i in range(15):
        total = total + rsb_kv[i]
    kvown[...] = total.astype(bf16).astype(f32)
    for i, step in enumerate(AROUND):
        peer = 2 * step_by(chip, step) + core
        send(kvown, kvall.at[chip], send_sem.at[3], kv_recv.at[1], peer).start()
    kvall[chip] = kvown[...]
    attend(range(64, 128), kc, vc, qs, nv, ks0, ks1, po, pm, ps)

    for i in range(0, 15, 2):
        group = range(i, min(i + 2, 15))
        heads = {k: step_by(chip, AROUND[k]) for k in group}
        for k in group:
            fold(heads[k], sel, selt, vs, po, pm, ps, msg, stats)
        for k in group:
            for c in range(2):
                at = 2 * k + c
                peer = 2 * heads[k] + (other if c else core)
                send(msg.at[peer], rmsg.at[at], send_sem.at[4], o_recv.at[0], peer).start()
                send(stats.at[heads[k]], rstats.at[at], send_sem.at[5], o_recv.at[1], peer).start()
    fold(chip, sel, selt, vs, po, pm, ps, msg, stats)
    send(msg.at[sibling], rmsg.at[30], send_sem.at[4], o_recv.at[0], sibling).start()
    send(stats.at[chip], rstats.at[30], send_sem.at[5], o_recv.at[1], sibling).start()
    rmsg[31] = msg[me]
    rstats[31] = stats[chip]
    landed(kvall.at[pl.ds(0, 15)], kv_recv.at[1])
    own, new_value = own_score(chip, qown, kvall)
    landed(rstats.at[pl.ds(0, 31)], o_recv.at[1])
    landed(rmsg.at[pl.ds(0, 31)], o_recv.at[0])
    ctx_own[...] = finish(core, rmsg, rstats, own, new_value, flat, turned)

    for i, step in enumerate(AROUND):
        peer = 2 * step_by(chip, step) + core
        send(ctx_own, ctx_all.at[chip], send_sem.at[6], c_recv.at[GROUP[i]], peer).start()
    share.wait_send()
    landed(wo.at[other], sib_sem.at[5])

    def project_half(c, h, context):
        rows = pl.ds(pl.multiple_of(h * HD, HD), HD)
        return jnp.dot(context, wo[c, rows, :], preferred_element_type=f32)

    sources = [step_by(chip, step, back=True) for step in AROUND]
    result = [project_half(c, chip, ctx_own[...]) for c in range(2)]
    mine = 4 * core + col
    for g in (2, 1, 0):
        landed(ctx_all.at[pl.ds(0, len(GROUPS[g]))], c_recv.at[g])
        for c in range(2):
            for i in GROUPS[g]:
                result[c] = result[c] + project_half(c, sources[i], ctx_all[sources[i]])
            if g == 0:
                xsend[c] = result[c].astype(bf16)
                for k in COLUMN:
                    send(xsend.at[c], xrecv.at[mine], send_sem.at[7], x_recv.at[0], 2 * chip + c, lax.rem(col + k, 4)).start()

    send(xsend.at[other], xrecv.at[mine], send_sem.at[7], x_recv.at[0], sibling).start()
    xrecv[mine] = xsend[core]
    landed(xrecv.at[pl.ds(0, 7)], x_recv.at[0])
    for c in range(2):
        result = xrecv[4 * c].astype(f32)
        for k in range(1, 4):
            result = result + xrecv[4 * c + k].astype(f32)
        out_ref[32 * c : 32 * c + 32] = result.astype(bf16)

    swap.wait_send()
    swap_kv.wait_send()
    left(rsb, send_sem.at[0])
    left(qall.at[pl.ds(0, 31)], send_sem.at[1])
    left(rsb_kv, send_sem.at[2])
    left(kvall.at[pl.ds(0, 15)], send_sem.at[3])
    left(rmsg.at[pl.ds(0, 31)], send_sem.at[4])
    left(rstats.at[pl.ds(0, 31)], send_sem.at[5])
    left(ctx_all.at[pl.ds(0, 15)], send_sem.at[6])
    left(xrecv.at[pl.ds(0, 7)], send_sem.at[7])


def body(
    hidden_in, w_query, w_keyval, w_out, key_cache, value_cache, key_scale, value_scale, page_counts, slot_pages, trim
):
    vmem = pltpu.VMEM
    dma = pltpu.SemaphoreType.DMA
    return pl.pallas_call(
        kernel,
        out_shape=jax.ShapeDtypeStruct((64, 256), bf16),
        in_specs=[pl.BlockSpec(memory_space=pltpu.HBM)] * 11,
        out_specs=pl.BlockSpec(memory_space=pltpu.VMEM),
        scratch_shapes=[
            vmem((64, 256), bf16), vmem((256, 2048), bf16), vmem((256, 512), bf16), vmem((2, 2048, 256), bf16),
            vmem((128, PAGE, 256), bf16), vmem((128, PAGE, 256), bf16), vmem((2, 128), f32), vmem((2, 128), f32),
            vmem((1, 64), jnp.int32), vmem((1, 128), jnp.int32), vmem((1, 64), jnp.int32),
            vmem((2, 16, 32, HD), f32), vmem((16, 32, HD), f32), vmem((15, 32, HD), f32),
            vmem((2, 16, 8, HD), f32), vmem((16, 8, HD), f32), vmem((15, 8, HD), f32),
            vmem((32, HD), bf16), vmem((8, HD), f32), vmem((32, 32, HD), bf16), vmem((16, 8, HD), f32),
            vmem((2048, HD), f32), vmem((2048, HD), f32), vmem((2048, HD), f32), vmem((2048, HD), f32),
            vmem((128, 128), f32), vmem((64, 128), bf16), vmem((128, 128), f32),
            vmem((128, 128), f32), vmem((128, 128), f32), vmem((2, 128, 128), f32),
            vmem((32, 32, HD), bf16), vmem((32, 32, HD), bf16), vmem((16, 1, 128), f32), vmem((32, 1, 128), f32),
            vmem((128, 128), f32), vmem((128, 128), f32),
            vmem((32, HD), bf16), vmem((16, 32, HD), bf16), vmem((2, 32, 256), bf16), vmem((8, 32, 256), bf16),
            dma((11,)), dma((6,)), dma((8,)), dma((3,)), dma((3,)), dma((2,)), dma((2,)), dma((3,)), dma((1,)),
            pltpu.SemaphoreType.REGULAR,
        ],
        compiler_params=pltpu.CompilerParams(collective_id=0, has_side_effects=True, vmem_limit_bytes=63 << 20),
        cost_estimate=pl.CostEstimate(flops=300_000_000, bytes_accessed=20_000_000, transcendentals=300_000),
    )(
        hidden_in, w_query, w_keyval, w_out, key_cache, value_cache, key_scale.T, value_scale.T,
        page_counts.reshape(1, 64), slot_pages.reshape(1, 128), trim.reshape(1, 64),
    )


def solution(mesh):
    return jax.shard_map(
        body,
        mesh=mesh,
        in_specs=(
            P(None, "seq"),
            P("seq", "head"),
            P("seq", "head"),
            P("head", "seq"),
            P("seq", None, "head"),
            P("seq", None, "head"),
            P("seq", "head"),
            P("seq", "head"),
            P(),
            P("seq"),
            P(),
        ),
        out_specs=P(None, "seq"),
        check_vma=False,
    )
```
